128 devices in a mesh: node: 8 (over y, core), local: 16 (over x, z).
Axes of the slice: x: 4, y: 4, z: 4, core: 2. Of those that a mesh axis runs over, the one named last changes fastest.
Arguments:
- tokens: bfloat16 [16384, 3584], P(('node', 'local')), may hold values from -6 to 6
- cotangent: bfloat16 [16384, 3584], P(('node', 'local')), may hold values from -6 to 6
- routes: int32 [16384, 2], P(('node', 'local')), may hold values from 0 to 31, as said below
- route_gates: float32 [16384, 2], P(('node', 'local')), may hold values from 0.2 to 1
- route_slots: int32 [16384, 2], P(('node', 'local')), may hold values from 0 to 8, as said below
- w_gate: bfloat16 [65536, 3584], P(('node', 'local')), may hold values from -0.09375 to 0.09375
- w_up: bfloat16 [65536, 3584], P(('node', 'local')), may hold values from -0.09375 to 0.09375
- w_down: bfloat16 [65536, 3584], P(('node', 'local')), may hold values from -0.125 to 0.125
Outputs:
- grad_tokens: bfloat16 [16384, 3584], P(('node', 'local'))
- grad_gate: bfloat16 [65536, 3584], P(('node', 'local'))
- grad_up: bfloat16 [65536, 3584], P(('node', 'local'))
- grad_down: bfloat16 [65536, 3584], P(('node', 'local'))
The draws below stay inside these ranges and needn't reach their ends.
Inputs may be any that keep to these rules, and one draw needn't show every extreme that they name: `routes`: each row names 2 different experts, both of one group: g*4 to g*4 + 3 for one g. `route_slots`: among the routes of one device's tokens to one expert, those under 8 take distinct values; the value 8 marks a route dropped for lack of room.
All inputs are finite; a program needn't handle non-finite values.
Results may differ from the reference program's by a relative error of at most 0.0064.
Values may be sent and summed in bfloat16 or wider, within the bound.
A program may use at most 192 MiB of HBM per device.

```python
import jax
import jax.numpy as jnp
from jax import lax

D = 3584
HID = 2048
EXP_NODE = 4
TOP = 2
TOK_DEV = 128
EXPERTS = 32
HDEV = 512
TOKENS = 16384
CAP = 8
N_LOCAL = 16
DEVICES = 128


def route_table(key):
    blocks = TOKENS // TOK_DEV
    groups = EXPERTS // EXP_NODE
    hot_count = 2 * CAP + 8
    keys = jax.random.split(key, 7)
    hot_group = jax.random.randint(keys[0], (), 0, groups)
    order = jax.vmap(lambda block_key: jax.random.permutation(block_key, TOK_DEV))(jax.random.split(keys[1], blocks))
    order = order.astype(jnp.int32)
    rotation = jax.random.randint(keys[2], (blocks, 1), 0, EXP_NODE)
    first_hot = (order % EXP_NODE + rotation) % EXP_NODE
    second_hot = (order % EXP_NODE + 1 + 2 * (order // EXP_NODE % 2) + rotation) % EXP_NODE
    shift_one = jax.random.randint(keys[3], (blocks, TOK_DEV), 0, groups - 1)
    shift_two = jax.random.randint(keys[4], (blocks, TOK_DEV), 0, groups - 1)
    rest_group = (hot_group + 1 + jnp.minimum(shift_one, shift_two)) % groups
    first_rest = jax.random.randint(keys[5], (blocks, TOK_DEV), 0, EXP_NODE)
    second_rest = (first_rest + 1 + jax.random.randint(keys[6], (blocks, TOK_DEV), 0, EXP_NODE - 1)) % EXP_NODE
    is_hot = order < hot_count
    group = jnp.where(is_hot, hot_group, rest_group)
    first = jnp.where(is_hot, first_hot, first_rest)
    second = jnp.where(is_hot, second_hot, second_rest)
    routes = jnp.stack([group * EXP_NODE + first, group * EXP_NODE + second], axis=-1).astype(jnp.int32)
    names = jnp.any(routes[..., None] == jnp.arange(EXPERTS, dtype=jnp.int32), axis=-2).astype(jnp.int32)
    inverse = jnp.argsort(order, axis=1).astype(jnp.int32)
    sorted_names = jnp.take_along_axis(names, jnp.broadcast_to(inverse[..., None], names.shape), axis=1)
    before = jnp.cumsum(sorted_names, axis=1) - sorted_names
    rank_token = jnp.take_along_axis(before, jnp.broadcast_to(order[..., None], names.shape), axis=1)
    slots = jnp.minimum(jnp.take_along_axis(rank_token, routes, axis=2), CAP).astype(jnp.int32)
    return (routes.reshape(TOKENS, 2), slots.reshape(TOKENS, 2))


def draw_routes(key, part):
    routes, slots = route_table(key)
    return routes


def draw_route_slots(key, part):
    routes, slots = route_table(key)
    return slots


def shard_levels(stream_key, dims, cuts, low, largest):
    factor_of, own = 1.0, jax.random.fold_in(stream_key, 6)
    for dim, shards_of in cuts:
        draws = jnp.exp(jax.random.uniform(jax.random.fold_in(own, dim), (shards_of,), jnp.float32, low / len(cuts), largest / len(cuts)))
        factor_of = factor_of * jnp.repeat(draws, dims[dim] // shards_of).reshape([-1 if axis == dim else 1 for axis in range(len(dims))])
    return factor_of


def bell_draw(own_key, dims, scale, limit, cuts=(), kind=jnp.bfloat16):
    values = scale * jax.random.normal(own_key, dims, jnp.float32)
    if cuts:
        values = values * shard_levels(own_key, dims, cuts, -0.22, 0.18)
    return jnp.clip(values, -limit, limit).astype(kind)


def setup_inputs(seed: int = 0) -> dict:
    splits = jax.random.split(jax.random.key(seed), 9)
    return {
        "tokens": bell_draw(splits[0], (TOKENS, D), 1.0, 6.0, ((0, 128),)),
        "cotangent": bell_draw(splits[1], (TOKENS, D), 1.0, 6.0, ((0, 128),)),
        "routes": draw_routes(jax.random.fold_in(splits[8], 71), 0),
        "route_gates": jnp.clip(0.2 + 0.8 * jax.random.uniform(splits[3], (TOKENS, TOP), jnp.float32) ** shard_levels(splits[3], (TOKENS, TOP), ((0, 128),), -0.2, 0.2), 0.2, 1.0),
        "route_slots": draw_route_slots(jax.random.fold_in(splits[8], 71), 0),
        "w_gate": bell_draw(splits[5], (EXPERTS * HID, D), D ** -0.5, 0.09375, ((0, 128),)),
        "w_up": bell_draw(splits[6], (EXPERTS * HID, D), D ** -0.5, 0.09375, ((0, 128),)),
        "w_down": bell_draw(splits[7], (EXPERTS * HID, D), HID ** -0.5, 0.125, ((0, 128),)),
    }


def reference(tokens, cotangent, routes, route_gates, route_slots, w_gate, w_up, w_down):
    split_count = N_LOCAL // EXP_NODE
    buffer_rows = DEVICES * CAP
    route_count = TOKENS * TOP
    kept_mask = route_slots < CAP
    gated = (route_gates[:, :, None] * cotangent[:, None, :].astype(jnp.float32)).astype(jnp.bfloat16)
    source_dev = (jnp.arange(TOKENS, dtype=jnp.int32) // TOK_DEV)[:, None]
    target = jnp.where(kept_mask, routes * buffer_rows + source_dev * CAP + route_slots, EXPERTS * buffer_rows)
    slot_table = jnp.full((EXPERTS * buffer_rows,), route_count, jnp.int32)
    slot_table = slot_table.at[target.reshape(-1)].set(jnp.arange(route_count, dtype=jnp.int32), mode="drop")
    slot_table = slot_table.reshape(EXPERTS, buffer_rows)
    token_pad = jnp.concatenate([tokens, jnp.zeros((1, D), jnp.bfloat16)], axis=0)
    grad_pad = jnp.concatenate([gated.reshape(route_count, D), jnp.zeros((1, D), jnp.bfloat16)], axis=0)

    def one_expert(grad_total, inputs):
        row_index, expert_gate, expert_up, expert_down = inputs
        expert_rows = token_pad[row_index // TOP]
        expert_grads = grad_pad[row_index]
        pre_gate = jnp.dot(expert_rows, expert_gate.T, preferred_element_type=jnp.float32)
        pre_up = jnp.dot(expert_rows, expert_up.T, preferred_element_type=jnp.float32)
        sigmoid_gate = jax.nn.sigmoid(pre_gate)
        active = pre_gate * sigmoid_gate
        hidden = (active * pre_up).astype(jnp.bfloat16)
        hidden_grad = jnp.dot(expert_grads, expert_down.T, preferred_element_type=jnp.float32)
        gate_grad = (hidden_grad * pre_up * sigmoid_gate * (1.0 + pre_gate * (1.0 - sigmoid_gate))).astype(jnp.bfloat16)
        up_grad = (hidden_grad * active).astype(jnp.bfloat16)
        down_wgrad = jnp.dot(hidden.T, expert_grads, preferred_element_type=jnp.float32).astype(jnp.bfloat16)
        gate_wgrad = jnp.dot(gate_grad.T, expert_rows, preferred_element_type=jnp.float32).astype(jnp.bfloat16)
        up_wgrad = jnp.dot(up_grad.T, expert_rows, preferred_element_type=jnp.float32).astype(jnp.bfloat16)
        summed = jnp.zeros((buffer_rows, D), jnp.float32)
        for piece_index in range(split_count):
            low_edge = piece_index * HDEV
            high_edge = low_edge + HDEV
            partial_term = jnp.dot(gate_grad[:, low_edge:high_edge], expert_gate[low_edge:high_edge], preferred_element_type=jnp.float32)
            partial_term = partial_term + jnp.dot(up_grad[:, low_edge:high_edge], expert_up[low_edge:high_edge], preferred_element_type=jnp.float32)
            rounded = lax.optimization_barrier(partial_term.astype(jnp.bfloat16))
            summed = summed + rounded.astype(jnp.float32)
        grad_total = grad_total.at[row_index // TOP].add(summed)
        return grad_total, (gate_wgrad, up_wgrad, down_wgrad)

    zero_total = jnp.zeros((TOKENS + 1, D), jnp.float32)
    stacked = (slot_table, w_gate.reshape(EXPERTS, HID, D), w_up.reshape(EXPERTS, HID, D), w_down.reshape(EXPERTS, HID, D))
    grad_total, (gate_all, up_all, down_all) = lax.scan(one_expert, zero_total, stacked)
    return (grad_total[:TOKENS].astype(jnp.bfloat16), gate_all.reshape(EXPERTS * HID, D), up_all.reshape(EXPERTS * HID, D), down_all.reshape(EXPERTS * HID, D))
```

```python
import jax
import jax.numpy as jnp
from jax import lax
from jax.experimental import pallas as pl
from jax.experimental.pallas import tpu as pltpu
from jax.sharding import PartitionSpec as P

MESH = pl.DeviceIdType.MESH
BF16, F32 = jnp.bfloat16, jnp.float32
CAP = 8
TOK = 128
D = 3584
HDEV = 512
ROWS = 256
BLK = 16
TILE = 512
TILES = D // TILE
NT = (((1,), (1,)), ((), ()))
NN = (((1,), (0,)), ((), ()))


def mm(a, b, dims=NN):
    return lax.dot_general(a, b, dims, preferred_element_type=F32)


def mod4(v):
    return lax.rem(v, 4)


def kernel(
    tok, cot, routes, slots, gates, wg_h, wu_h, wd_h,
    out_tok, og_h, ou_h, od_h,
    wg, wu, wd, xs, gs, snd, tok_o, cot_o, meta, onehot, ret,
    swap_snd, swap_rcv, sum_snd, sum_rcv, ht, ggt, ugt, gg, ug, stage,
    w_sem, cx_send, cx_recv, m_send, m_recv, own_sem, d_send, d_recv,
    z_send, z_recv, f_send, r_send, r_recv, rown_sem,
    t_send, t_recv, o_send, o_recv, st_sem,
):
    node, local = lax.axis_index("node"), lax.axis_index("local")
    y, c = lax.div(node, 2), lax.rem(node, 2)
    x, z = lax.div(local, 4), lax.rem(local, 4)

    def dev(dx, dy, dz, flip=False):
        core = 1 - c if flip else c
        return (mod4(y + dy) * 2 + core, mod4(x + dx) * 4 + mod4(z + dz))

    def remote(src, dst, ssem, rsem, target):
        return pltpu.make_async_remote_copy(
            src_ref=src, dst_ref=dst, send_sem=ssem, recv_sem=rsem,
            device_id=target, device_id_type=MESH,
        )

    here = dev(0, 0, 0, True)

    def wait_recv(ref, sem):
        remote(ref, ref, sem, sem, here).wait_recv()

    def wait_send(ref, sem):
        remote(ref, ref, sem, sem, here).wait_send()

    loads = [
        pltpu.make_async_copy(src, dst, w_sem.at[k])
        for k, (src, dst) in enumerate(((wg_h, wg), (wu_h, wu), (wd_h, wd)))
    ]
    for load in loads:
        load.start()

    barrier = pltpu.get_barrier_semaphore()

    def greet(k, carry):
        pl.semaphore_signal(
            barrier, inc=1, device_id=dev(lax.rem(k, 4), lax.div(k, 4), 0), device_id_type=MESH
        )
        return carry

    lax.fori_loop(1, 16, greet, 0)
    for dz in (1, 2, 3):
        pl.semaphore_signal(barrier, inc=1, device_id=dev(0, 0, dz), device_id_type=MESH)
    pl.semaphore_signal(barrier, inc=1, device_id=here, device_id_type=MESH)

    lane = lax.broadcasted_iota(jnp.int32, (TOK, 128), 1)
    target = jnp.where(slots[...] < CAP, routes[...] * CAP + slots[...], -1).astype(F32)
    gate = gates[...]
    meta[0, 0] = jnp.where(
        lane == 0, target[:, 0:1],
        jnp.where(lane == 1, target[:, 1:2], jnp.where(lane == 2, gate[:, 0:1], gate[:, 1:2])),
    )
    pl.semaphore_wait(barrier, 19)

    swaps = [
        remote(src, dst, cx_send.at[k], cx_recv.at[k], here)
        for k, (src, dst) in enumerate(
            ((meta.at[0, 0], meta.at[0, 1]), (tok, tok_o), (cot, cot_o))
        )
    ]
    for swap in swaps:
        swap.start()

    def row_target(r, core):
        e = (mod4(y + (r >> 6)) * 2 + c) * 4 + mod4(x + ((r >> 4) & 3))
        return jnp.where(((r >> 3) & 1) == core, e * CAP + (r & 7), -2).astype(F32)

    swaps[0].wait_recv()
    metas = [
        remote(meta.at[0], meta.at[4 - dz], m_send.at[dz - 1], m_recv.at[3 - dz], dev(0, 0, dz))
        for dz in (1, 2, 3)
    ]
    for m in metas:
        m.start()

    row_ids = lax.broadcasted_iota(jnp.int32, (ROWS, TOK), 0)
    row_gate = jnp.zeros((ROWS, 1), F32)
    for k, core in enumerate((c, 1 - c)):
        want = row_target(row_ids, core)
        mt = meta[0, k].T
        hit0, hit1 = want == mt[0:1, :], want == mt[1:2, :]
        onehot[k] = (jnp.where(hit0, 1.0, 0.0) + jnp.where(hit1, 1.0, 0.0)).astype(BF16)
        picked = jnp.where(hit0, mt[2:3, :], 0.0) + jnp.where(hit1, mt[3:4, :], 0.0)
        row_gate = row_gate + jnp.sum(picked, axis=1, keepdims=True)

    own_rows = pl.ds(pl.multiple_of((y * 4 + x) * BLK, BLK), BLK)

    def dispatch(a, buf):
        pltpu.make_async_copy(snd.at[a, pl.ds(0, BLK)], buf.at[own_rows], own_sem.at[a]).start()

        def send(k, carry):
            i, j = lax.div(k, 4), lax.rem(k, 4)
            remote(
                snd.at[a, pl.ds(pl.multiple_of(k * BLK, BLK), BLK)], buf.at[own_rows],
                d_send.at[a], d_recv.at[a, i], dev(j, i, 0),
            ).start()
            return carry

        lax.fori_loop(1, 16, send, 0)

    def tiled(body):
        def step(t, carry):
            body(pl.ds(pl.multiple_of(t * TILE, TILE), TILE))
            return carry

        lax.fori_loop(0, TILES, step, 0)

    swaps[1].wait_recv()

    def build_x(cols):
        rows = mm(onehot[0], tok[:, cols]) + mm(onehot[1], tok_o[:, cols])
        snd[0, :, cols] = rows.astype(BF16)

    tiled(build_x)
    dispatch(0, xs)
    swaps[2].wait_recv()

    def build_g(cols):
        rows = mm(onehot[0], cot[:, cols]) + mm(onehot[1], cot_o[:, cols])
        snd[1, :, cols] = (row_gate * rows).astype(BF16)

    tiled(build_g)
    dispatch(1, gs)

    def group(i):
        return pl.multiple_of(mod4(y + 4 - i) * 64, 64)

    bufs = (xs, gs)
    for i in range(4):
        off = group(i)
        for a, buf in enumerate(bufs):
            if i == 0:
                pltpu.make_async_copy(
                    snd.at[a, pl.ds(0, BLK)], buf.at[own_rows], own_sem.at[a]
                ).wait()
            wait_recv(buf.at[pl.ds(0, 48 if i == 0 else 64)], d_recv.at[a, i])
            for k, (dz, slot) in enumerate(((1, 3), (3, 1))):
                remote(
                    buf.at[pl.ds(off, 64)], buf.at[pl.ds(off + slot * ROWS, 64)],
                    z_send.at[k, a, i], z_recv.at[slot - 1, a, i], dev(0, 0, dz),
                ).start()

    def wait_z(slot, a, i):
        wait_recv(bufs[a].at[pl.ds(0, 64)], z_recv.at[slot - 1, a, i])

    def forward(i):
        off = group(i)
        for a, slot, dz in ((0, 3, 1), (1, 1, 3)):
            wait_z(slot, a, i)
            remote(
                bufs[a].at[pl.ds(off + slot * ROWS, 64)], bufs[a].at[pl.ds(off + 2 * ROWS, 64)],
                f_send.at[a, i], z_recv.at[1, a, i], dev(0, 0, dz),
            ).start()

    def expert_pass(d, slot):
        rows = pl.ds(d * ROWS, ROWS)

        def hidden_part(h, carry):
            hid = pl.ds(pl.multiple_of(h * 256, 256), 256)
            pre_gate = mm(wg[hid, :], xs[rows, :], NT)
            pre_up = mm(wu[hid, :], xs[rows, :], NT)
            hidden_grad = mm(wd[hid, :], gs[rows, :], NT)
            sig = jax.nn.sigmoid(pre_gate)
            active = pre_gate * sig
            ht[hid, rows] = (active * pre_up).astype(BF16)
            gate_grad = hidden_grad * pre_up * sig * (1.0 + pre_gate * (1.0 - sig))
            up_grad = hidden_grad * active
            ggt[hid, rows] = gate_grad.astype(BF16)
            ugt[hid, rows] = up_grad.astype(BF16)
            gg[:, hid] = gate_grad.T.astype(BF16)
            ug[:, hid] = up_grad.T.astype(BF16)
            return carry

        lax.fori_loop(0, HDEV // 256, hidden_part, 0)

        def part(cols):
            snd[slot, :, cols] = (mm(gg[...], wg[:, cols]) + mm(ug[...], wu[:, cols])).astype(BF16)

        tiled(part)
        own = pltpu.make_async_copy(
            snd.at[slot, own_rows], ret.at[pl.ds(d * ROWS, BLK)], rown_sem.at[d]
        )
        own.start()

        def send(k, carry):
            i, j = lax.div(k, 4), lax.rem(k, 4)
            row = pl.multiple_of((mod4(y + 4 - i) * 4 + mod4(x + 4 - j)) * BLK, BLK)
            remote(
                snd.at[slot, pl.ds(row, BLK)],
                ret.at[pl.ds(pl.multiple_of(d * ROWS + k * BLK, BLK), BLK)],
                r_send.at[d], r_recv.at[d], dev(4 - j, 4 - i, 0),
            ).start()
            return carry

        lax.fori_loop(1, 16, send, 0)
        own.wait()

    def returned(d, slot):
        wait_send(snd.at[slot, pl.ds(0, 240)], r_send.at[d])

    def swap_copy(d):
        return remote(swap_snd.at[d], swap_rcv.at[d], t_send.at[d], t_recv.at[d], here)

    def sum_copy(d):
        return remote(
            sum_snd.at[d], sum_rcv.at[3 - d], o_send.at[d - 1], o_recv.at[3 - d], dev(0, 0, d)
        )

    def combine(d):
        wait_recv(ret.at[pl.ds(d * ROWS, 240)], r_recv.at[d])
        if d:
            wait_recv(meta.at[d], m_recv.at[d - 1])
        col_ids = lax.broadcasted_iota(jnp.int32, (TOK, ROWS), 1)
        picks = []
        for k, core in enumerate((c, 1 - c)):
            want = row_target(col_ids, core)
            m = meta[d, k]
            pick = jnp.where(want == m[:, 0:1], 1.0, 0.0) + jnp.where(want == m[:, 1:2], 1.0, 0.0)
            picks.append(pick.astype(BF16))

        def sums(cols):
            rows = ret[pl.ds(d * ROWS, ROWS), cols]
            sum_snd[d, :, cols] = mm(picks[0], rows).astype(BF16)
            swap_snd[d, :, cols] = mm(picks[1], rows).astype(BF16)

        tiled(sums)
        swap_copy(d).start()

    def pass_on(d):
        swap_copy(d).wait_recv()

        def add(cols):
            both = sum_snd[d, :, cols].astype(F32) + swap_rcv[d, :, cols].astype(F32)
            sum_snd[d, :, cols] = both.astype(BF16)

        tiled(add)
        if d:
            sum_copy(d).start()

    forward(0)
    for load in loads:
        load.wait()
    for a in range(2):
        wait_send(snd.at[a, pl.ds(0, 240)], d_send.at[a])
    expert_pass(0, 0)
    for i in range(1, 4):
        forward(i)
    for i in range(4):
        wait_z(3, 1, i)
    expert_pass(3, 1)
    for i in range(4):
        wait_z(1, 0, i)
    returned(0, 0)
    expert_pass(1, 0)
    combine(0)
    pass_on(0)
    for i in range(4):
        for a in range(2):
            wait_z(2, a, i)
    returned(3, 1)
    expert_pass(2, 1)
    combine(3)
    combine(1)
    pass_on(3)
    pass_on(1)

    jobs = ((ggt, xs, og_h), (ugt, xs, ou_h), (ht, gs, od_h))

    def stage_copy(t, n, slot):
        cols = pl.ds(pl.multiple_of(t * TILE, TILE), TILE)
        return pltpu.make_async_copy(stage.at[slot, n], jobs[n][2].at[:, cols], st_sem.at[slot, n])

    def wgrad(t, carry):
        slot = lax.rem(t, 2)
        cols = pl.ds(pl.multiple_of(t * TILE, TILE), TILE)
        for n, (left, right, _) in enumerate(jobs):

            @pl.when(t >= 2)
            def _():
                stage_copy(t - 2, n, slot).wait()

            stage[slot, n] = mm(left[...], right[:, cols]).astype(BF16)
            stage_copy(t, n, slot).start()
        return carry

    lax.fori_loop(0, TILES, wgrad, 0)

    combine(2)
    pass_on(2)
    for d in (3, 1, 2):
        wait_recv(sum_rcv.at[d - 1], o_recv.at[d - 1])

    def total(cols):
        acc = sum_snd[0, :, cols].astype(F32)
        for k in range(3):
            acc = acc + sum_rcv[k, :, cols].astype(F32)
        out_tok[:, cols] = acc.astype(BF16)

    tiled(total)

    for t in (TILES - 2, TILES - 1):
        for n in range(3):
            stage_copy(t, n, t % 2).wait()
    for swap in swaps:
        swap.wait_send()
    for m in metas:
        m.wait_send()
    for i in range(4):
        for a, buf in enumerate(bufs):
            for k in range(2):
                wait_send(buf.at[pl.ds(0, 64)], z_send.at[k, a, i])
            wait_send(buf.at[pl.ds(0, 64)], f_send.at[a, i])
    returned(1, 0)
    returned(2, 1)
    for d in range(4):
        swap_copy(d).wait_send()
        if d:
            sum_copy(d).wait_send()


def per_device(tokens, cotangent, routes, route_gates, route_slots, w_gate, w_up, w_down):
    vmem, hbm = pl.BlockSpec(memory_space=pltpu.VMEM), pl.BlockSpec(memory_space=pl.ANY)
    dma = pltpu.SemaphoreType.DMA
    grad = jax.ShapeDtypeStruct((HDEV, D), BF16)
    return pl.pallas_call(
        kernel,
        out_shape=(jax.ShapeDtypeStruct((TOK, D), BF16), grad, grad, grad),
        in_specs=[vmem] * 5 + [hbm] * 3,
        out_specs=(vmem, hbm, hbm, hbm),
        scratch_shapes=[
            pltpu.VMEM((HDEV, D), BF16),
            pltpu.VMEM((HDEV, D), BF16),
            pltpu.VMEM((HDEV, D), BF16),
            pltpu.VMEM((4 * ROWS, D), BF16),
            pltpu.VMEM((4 * ROWS, D), BF16),
            pltpu.VMEM((2, ROWS, D), BF16),
            pltpu.VMEM((TOK, D), BF16),
            pltpu.VMEM((TOK, D), BF16),
            pltpu.VMEM((4, 2, TOK, 128), F32),
            pltpu.VMEM((2, ROWS, TOK), BF16),
            pltpu.VMEM((4 * ROWS, D), BF16),
            pltpu.VMEM((4, TOK, D), BF16),
            pltpu.VMEM((4, TOK, D), BF16),
            pltpu.VMEM((4, TOK, D), BF16),
            pltpu.VMEM((3, TOK, D), BF16),
            pltpu.VMEM((HDEV, 4 * ROWS), BF16),
            pltpu.VMEM((HDEV, 4 * ROWS), BF16),
            pltpu.VMEM((HDEV, 4 * ROWS), BF16),
            pltpu.VMEM((ROWS, HDEV), BF16),
            pltpu.VMEM((ROWS, HDEV), BF16),
            pltpu.VMEM((2, 3, HDEV, TILE), BF16),
            dma((3,)), dma((3,)), dma((3,)), dma((3,)), dma((3,)),
            dma((2,)), dma((2,)), dma((2, 4)),
            dma((2, 2, 4)), dma((3, 2, 4)), dma((2, 4)),
            dma((4,)), dma((4,)), dma((4,)),
            dma((4,)), dma((4,)), dma((3,)), dma((3,)), dma((2, 3)),
        ],
        compiler_params=pltpu.CompilerParams(
            collective_id=0, has_side_effects=True, vmem_limit_bytes=63 * 2**20
        ),
        cost_estimate=pl.CostEstimate(
            flops=8 * 2 * 1024 * D * HDEV, bytes_accessed=6 * 2 * HDEV * D, transcendentals=1024 * HDEV
        ),
    )(tokens, cotangent, routes, route_slots, route_gates, w_gate, w_up, w_down)


def solution(mesh):
    spec = P(("node", "local"), None)
    return jax.shard_map(
        per_device, mesh=mesh, in_specs=(spec,) * 8, out_specs=(spec,) * 4, check_vma=False
    )
```

```python
import jax
import jax.numpy as jnp
from jax import lax
from jax.experimental import pallas as pl
from jax.experimental.pallas import tpu as pltpu
from jax.sharding import PartitionSpec as P

MESH = pl.DeviceIdType.MESH
BF16, F32 = jnp.bfloat16, jnp.float32
CAP = 8
TOK = 128
D = 3584
HDEV = 512
BLK = 16
ROWS = 256
HALF = 128
TILE = 512
NT = (((1,), (1,)), ((), ()))
NN = (((1,), (0,)), ((), ()))
STEPS = (
    (0, 0), (1, 0), (0, 1), (3, 0), (0, 3), (1, 1), (3, 3), (1, 3),
    (3, 1), (2, 0), (0, 2), (2, 1), (1, 2), (2, 3), (3, 2), (2, 2),
)
X_STEPS = sum(dx << (2 * q) for q, (dx, _) in enumerate(STEPS))
Y_STEPS = sum(dy << (2 * q) for q, (_, dy) in enumerate(STEPS))
PLACE = {0: (0, 128), 1: (256, 512), 3: (384, 640), 2: (768, 896)}
WHOLE = ((0, D),)
PIECES = ((0, 1536), (1536, 1024), (2560, 1024))


def signed(v):
    return v - (1 << 32) if v >= 1 << 31 else v


def mm(a, b, dims=NN):
    return lax.dot_general(a, b, dims, preferred_element_type=F32)


def mod4(v):
    return lax.rem(v, 4)


def tiled(body, start=0, size=D):
    def step(t, carry):
        body(pl.ds(pl.multiple_of(start + t * TILE, TILE), TILE))
        return carry

    lax.fori_loop(0, size // TILE, step, 0)


def place(d, q):
    return PLACE[d][q // 8] + q % 8 * BLK


def kernel(
    tok, cot, routes, slots, gates, wg_h, wu_h, wd_h,
    out_tok, og_h, ou_h, od_h,
    wg, wu, wd, xs, gs, snd, toks, cots, meta, onehot, picks, ret,
    swap_snd, swap_rcv, sum_snd, sum_rcv, ht, ggt, ugt, gg, ug, stage,
    w_sem, l_sem, cx_send, cx_recv, m_send, m_recv, own_sem, d_send, d_recv,
    z_send, z_recv, f_send, f_recv, r_send, r_recv, rown_sem,
    t_send, t_recv, o_send, o_recv, st_sem,
):
    node, local = lax.axis_index("node"), lax.axis_index("local")
    y, c = lax.div(node, 2), lax.rem(node, 2)
    x, z = lax.div(local, 4), lax.rem(local, 4)

    def dev(dx, dy, dz, flip=False):
        core = 1 - c if flip else c
        return (mod4(y + dy) * 2 + core, mod4(x + dx) * 4 + mod4(z + dz))

    def remote(src, dst, ssem, rsem, target):
        return pltpu.make_async_remote_copy(
            src_ref=src, dst_ref=dst, send_sem=ssem, recv_sem=rsem,
            device_id=target, device_id_type=MESH,
        )

    here = dev(0, 0, 0, True)

    def wait_recv(ref, sem):
        remote(ref, ref, sem, sem, here).wait_recv()

    def wait_send(ref, sem):
        remote(ref, ref, sem, sem, here).wait_send()

    mine = pl.ds(pl.multiple_of(c * TOK, TOK), TOK)
    own_loads = [
        pltpu.make_async_copy(src, dst.at[mine], l_sem.at[k])
        for k, (src, dst) in enumerate(((tok, toks), (cot, cots)))
    ]
    loads = [
        pltpu.make_async_copy(src, dst, w_sem.at[k])
        for k, (src, dst) in enumerate(((wg_h, wg), (wu_h, wu), (wd_h, wd)))
    ]
    for load in own_loads + loads:
        load.start()

    barrier = pltpu.get_barrier_semaphore()

    def greet(target):
        pl.semaphore_signal(barrier, inc=1, device_id=target, device_id_type=MESH)

    greet(here)
    for dx, dy in STEPS[1:]:
        greet(dev(dx, dy, 0))
    for dz in (1, 2, 3):
        greet(dev(0, 0, dz))

    line = lax.broadcasted_iota(jnp.int32, (8, TOK), 0)
    target = jnp.where(slots[...] < CAP, routes[...] * CAP + slots[...], -1).astype(F32)
    gate = gates[...]
    meta[0, c] = jnp.where(
        line == 0, target[0:1, :],
        jnp.where(line == 1, target[1:2, :], jnp.where(line == 2, gate[0:1, :], gate[1:2, :])),
    )
    pl.semaphore_wait(barrier, 19)

    swaps = [
        remote(src, dst, cx_send.at[k], cx_recv.at[k], here)
        for k, (src, dst) in enumerate(
            ((meta.at[0, c], meta.at[0, c]), (tok, toks.at[mine]), (cot, cots.at[mine]))
        )
    ]
    for swap in swaps:
        swap.start()

    def row_target(r, core):
        q2 = (r >> 4) * 2
        ey = mod4(y + ((jnp.int32(signed(Y_STEPS)) >> q2) & 3))
        ex = mod4(x + ((jnp.int32(signed(X_STEPS)) >> q2) & 3))
        e = (ey * 2 + c) * 4 + ex
        return jnp.where(((r >> 3) & 1) == core, e * CAP + (r & 7), -2).astype(F32)

    swaps[0].wait_recv()
    metas = [
        remote(meta.at[0], meta.at[4 - dz], m_send.at[dz - 1], m_recv.at[3 - dz], dev(0, 0, dz))
        for dz in (1, 2, 3)
    ]
    for m in metas:
        m.start()

    row_ids = lax.broadcasted_iota(jnp.int32, (ROWS, TOK), 0)
    row_gate = jnp.zeros((ROWS, 1), F32)
    for core in (0, 1):
        want = row_target(row_ids, core)
        mt = meta[0, core]
        hit0, hit1 = want == mt[0:1, :], want == mt[1:2, :]
        onehot[:, pl.ds(core * TOK, TOK)] = (
            jnp.where(hit0, 1.0, 0.0) + jnp.where(hit1, 1.0, 0.0)
        ).astype(BF16)
        picked = jnp.where(hit0, mt[2:3, :], 0.0) + jnp.where(hit1, mt[3:4, :], 0.0)
        row_gate = row_gate + jnp.sum(picked, axis=1, keepdims=True)

    for copy in own_loads:
        copy.wait()
    for swap in swaps[1:]:
        swap.wait_recv()

    bufs = (xs, gs)

    def own_copy(a):
        return pltpu.make_async_copy(
            snd.at[a, pl.ds(0, BLK)], bufs[a].at[pl.ds(0, BLK)], own_sem.at[a]
        )

    for half in range(2):
        rows = pl.ds(half * HALF, HALF)
        half_gate = row_gate[half * HALF : half * HALF + HALF]

        def build(cols, rows=rows, half_gate=half_gate):
            snd[0, rows, cols] = mm(onehot[rows, :], toks[:, cols]).astype(BF16)
            snd[1, rows, cols] = (half_gate * mm(onehot[rows, :], cots[:, cols])).astype(BF16)

        tiled(build)
        for q in range(half * 8, half * 8 + 8):
            dx, dy = STEPS[q]
            for a in range(2):
                if q == 0:
                    own_copy(a).start()
                else:
                    remote(
                        snd.at[a, pl.ds(q * BLK, BLK)], bufs[a].at[pl.ds(place(0, q), BLK)],
                        d_send.at[a], d_recv.at[q], dev(dx, dy, 0),
                    ).start()

    for q in range(16):
        if q == 0:
            for a in range(2):
                own_copy(a).wait()
        else:
            wait_recv(xs.at[pl.ds(0, 2 * BLK)], d_recv.at[q])
        for dz, slot in ((1, 3), (3, 1)):
            for a in range(2):
                remote(
                    bufs[a].at[pl.ds(place(0, q), BLK)], bufs[a].at[pl.ds(place(slot, q), BLK)],
                    z_send.at[dz // 2], z_recv.at[slot // 2, q], dev(0, 0, dz),
                ).start()

    def forward(q):
        for a, slot, dz in ((0, 3, 1), (1, 1, 3)):
            wait_recv(xs.at[pl.ds(0, 2 * BLK)], z_recv.at[slot // 2, q])
            remote(
                bufs[a].at[pl.ds(place(slot, q), BLK)], bufs[a].at[pl.ds(place(2, q), BLK)],
                f_send.at[a], f_recv.at[q], dev(0, 0, dz),
            ).start()

    def hidden_pass(row, count, at):
        rows, to = pl.ds(row, count), pl.ds(at, count)

        def step(h, carry):
            hid = pl.ds(pl.multiple_of(h * 256, 256), 256)
            pre_gate = mm(wg[hid, :], xs[rows, :], NT)
            pre_up = mm(wu[hid, :], xs[rows, :], NT)
            hidden_grad = mm(wd[hid, :], gs[rows, :], NT)
            sig = jax.nn.sigmoid(pre_gate)
            active = pre_gate * sig
            ht[hid, rows] = (active * pre_up).astype(BF16)
            gate_grad = hidden_grad * pre_up * sig * (1.0 + pre_gate * (1.0 - sig))
            up_grad = hidden_grad * active
            ggt[hid, rows] = gate_grad.astype(BF16)
            ugt[hid, rows] = up_grad.astype(BF16)
            gg[to, hid] = gate_grad.T.astype(BF16)
            ug[to, hid] = up_grad.T.astype(BF16)
            return carry

        lax.fori_loop(0, HDEV // 256, step, 0)

    def give_back(slot, at, count, blocks, sem, start=0, size=D):
        to = pl.ds(at, count)

        def part(cols):
            snd[slot, to, cols] = (
                mm(gg[to, :], wg[:, cols]) + mm(ug[to, :], wu[:, cols])
            ).astype(BF16)

        tiled(part, start, size)
        cols = pl.ds(start, size)
        own = []
        for row, d, q in blocks:
            src = snd.at[slot, pl.ds(row, BLK), cols]
            dst = ret.at[pl.ds(d * ROWS + q * BLK, BLK), cols]
            if q == 0:
                own.append(pltpu.make_async_copy(src, dst, rown_sem.at[d]))
                own[-1].start()
            else:
                dx, dy = STEPS[q]
                remote(
                    src, dst, r_send.at[sem], r_recv.at[d, sem], dev(4 - dx, 4 - dy, 0)
                ).start()
        for copy in own:
            copy.wait()

    def part_ids(d):
        return (3, 4, 5) if d == 2 else (d // 2 + (d > 0),)

    def spans(d):
        return PIECES if d == 2 else WHOLE

    def swap_copy(d, k):
        cols, i = pl.ds(*spans(d)[k]), part_ids(d)[k]
        return remote(
            swap_snd.at[d, :, cols], swap_rcv.at[d, :, cols], t_send.at[i], t_recv.at[i], here
        )

    def sum_copy(d, k):
        cols, i, o = pl.ds(*spans(d)[k]), part_ids(d)[k], part_ids((4 - d) % 4)[k]
        return remote(
            sum_snd.at[d, :, cols], sum_rcv.at[3 - d, :, cols],
            o_send.at[i], o_recv.at[o], dev(0, 0, d),
        )

    def prepare(d):
        if d:
            wait_recv(meta.at[d], m_recv.at[d - 1])
        col_ids = lax.broadcasted_iota(jnp.int32, (TOK, ROWS), 1)
        for k, core in enumerate((c, 1 - c)):
            want = row_target(col_ids, core)
            m = meta[d, core].T
            pick = jnp.where(want == m[:, 0:1], 1.0, 0.0) + jnp.where(want == m[:, 1:2], 1.0, 0.0)
            picks[d, k] = pick.astype(BF16)

    def combine(d, k):
        start, size = spans(d)[k]

        def sums(cols):
            rows = ret[pl.ds(d * ROWS, ROWS), cols]
            sum_snd[d, :, cols] = mm(picks[d, 0], rows).astype(BF16)
            swap_snd[d, :, cols] = mm(picks[d, 1], rows).astype(BF16)

        tiled(sums, start, size)
        swap_copy(d, k).start()

    def pass_on(d, k):
        start, size = spans(d)[k]
        swap_copy(d, k).wait_recv()

        def add(cols):
            both = sum_snd[d, :, cols].astype(F32) + swap_rcv[d, :, cols].astype(F32)
            sum_snd[d, :, cols] = both.astype(BF16)

        tiled(add, start, size)
        if d:
            sum_copy(d, k).start()

    def wait_back(d, rows, sem, start=0, size=D):
        wait_recv(ret.at[pl.ds(0, rows), pl.ds(start, size)], r_recv.at[d, sem])

    for q in range(8):
        forward(q)
    for load in loads:
        load.wait()
    for a in range(2):
        wait_send(snd.at[a, pl.ds(0, 240)], d_send.at[a])
    hidden_pass(0, ROWS, 0)
    give_back(0, 0, ROWS, [(q * BLK, 0, q) for q in range(16)], 0)
    hidden_pass(256, ROWS, 0)
    near = [(q % 8 * BLK + k * HALF, d, q) for k, d in enumerate((1, 3)) for q in range(16)]
    give_back(1, 0, ROWS, [b for b in near if b[2] < 8], 1)
    for d in range(4):
        prepare(d)
    for q in range(8, 16):
        forward(q)

    wait_send(snd.at[0, pl.ds(0, 240)], r_send.at[0])
    hidden_pass(512, ROWS, 0)
    give_back(0, 0, ROWS, [b for b in near if b[2] >= 8], 2)
    wait_back(0, 240, 0)
    combine(0, 0)

    for q in range(8):
        wait_recv(xs.at[pl.ds(0, 2 * BLK)], f_recv.at[q])
    pass_on(0, 0)
    wait_send(snd.at[1, pl.ds(0, 224)], r_send.at[1])
    hidden_pass(768, HALF, 0)
    give_back(1, 0, HALF, [(q * BLK, 2, q) for q in range(8)], 3)
    for d in (1, 3):
        wait_back(d, 112, 1)
        wait_back(d, 128, 2)
        combine(d, 0)
    for d in (1, 3):
        pass_on(d, 0)
    for q in range(8, 16):
        wait_recv(xs.at[pl.ds(0, 2 * BLK)], f_recv.at[q])
    hidden_pass(896, HALF, HALF)
    for k, span in enumerate(PIECES):
        give_back(1, HALF, HALF, [(q * BLK, 2, q) for q in range(8, 16)], 4 + k, *span)

    jobs = ((ggt, xs, og_h), (ugt, xs, ou_h), (ht, gs, od_h))

    def stage_copy(t, n):
        return pltpu.make_async_copy(
            stage.at[t % 2, n], jobs[n][2].at[:, pl.ds(t * TILE, TILE)], st_sem.at[t % 2, n]
        )

    def wgrad(t):
        for n, (left, right, _) in enumerate(jobs):
            if t >= 2:
                stage_copy(t - 2, n).wait()
            stage[t % 2, n] = mm(left[...], right[:, pl.ds(t * TILE, TILE)]).astype(BF16)
            stage_copy(t, n).start()

    def last(k):
        if k == 0:
            wait_back(2, 112, 3)
        wait_back(2, 128, 4 + k, *PIECES[k])
        combine(2, k)

    wgrad(0)
    wgrad(1)
    wgrad(2)
    last(0)
    wgrad(3)
    pass_on(2, 0)
    last(1)
    wgrad(4)
    pass_on(2, 1)
    last(2)
    wgrad(5)
    pass_on(2, 2)
    wgrad(6)

    for d in (1, 3):
        wait_recv(sum_rcv.at[d - 1], o_recv.at[part_ids(d)[0]])
    for k, (start, size) in enumerate(PIECES):
        wait_recv(sum_rcv.at[1, :, pl.ds(start, size)], o_recv.at[part_ids(2)[k]])

        def total(cols):
            acc = sum_snd[0, :, cols].astype(F32)
            for n in range(3):
                acc = acc + sum_rcv[n, :, cols].astype(F32)
            out_tok[:, cols] = acc.astype(BF16)

        tiled(total, start, size)

    for t in (5, 6):
        for n in range(3):
            stage_copy(t, n).wait()
    for swap in swaps:
        swap.wait_send()
    for m in metas:
        m.wait_send()
    for k in range(2):
        wait_send(xs.at[pl.ds(0, 512)], z_send.at[k])
        wait_send(xs.at[pl.ds(0, ROWS)], f_send.at[k])
    wait_send(snd.at[0, pl.ds(0, ROWS)], r_send.at[2])
    wait_send(snd.at[0, pl.ds(0, 112)], r_send.at[3])
    for k, (start, size) in enumerate(PIECES):
        wait_send(snd.at[0, pl.ds(0, HALF), pl.ds(start, size)], r_send.at[4 + k])
    for d in range(4):
        for k in range(len(spans(d))):
            swap_copy(d, k).wait_send()
            if d:
                sum_copy(d, k).wait_send()


def per_device(tokens, cotangent, routes, route_gates, route_slots, w_gate, w_up, w_down):
    vmem, hbm = pl.BlockSpec(memory_space=pltpu.VMEM), pl.BlockSpec(memory_space=pl.ANY)
    dma = pltpu.SemaphoreType.DMA
    grad = jax.ShapeDtypeStruct((HDEV, D), BF16)

    def room(*shape):
        return pltpu.VMEM(shape, BF16)

    return pl.pallas_call(
        kernel,
        out_shape=(jax.ShapeDtypeStruct((TOK, D), BF16), grad, grad, grad),
        in_specs=[hbm] * 2 + [vmem] * 3 + [hbm] * 3,
        out_specs=(vmem, hbm, hbm, hbm),
        scratch_shapes=[
            room(HDEV, D), room(HDEV, D), room(HDEV, D),
            room(4 * ROWS, D), room(4 * ROWS, D), room(2, ROWS, D),
            room(2 * TOK, D), room(2 * TOK, D),
            pltpu.VMEM((4, 2, 8, TOK), F32), room(ROWS, 2 * TOK), room(4, 2, TOK, ROWS),
            room(4 * ROWS, D),
            room(4, TOK, D), room(4, TOK, D), room(4, TOK, D), room(3, TOK, D),
            room(HDEV, 4 * ROWS), room(HDEV, 4 * ROWS), room(HDEV, 4 * ROWS),
            room(ROWS, HDEV), room(ROWS, HDEV), room(2, 3, HDEV, TILE),
            dma((3,)), dma((2,)), dma((3,)), dma((3,)), dma((3,)), dma((3,)), dma((2,)),
            dma((2,)), dma((16,)),
            dma((2,)), dma((2, 16)), dma((2,)), dma((16,)), dma((7,)), dma((4, 7)), dma((4,)),
            dma((6,)), dma((6,)), dma((6,)), dma((6,)), dma((2, 3)),
        ],
        compiler_params=pltpu.CompilerParams(
            collective_id=0, has_side_effects=True, vmem_limit_bytes=63 * 2**20
        ),
        cost_estimate=pl.CostEstimate(
            flops=8 * 2 * 1024 * D * HDEV, bytes_accessed=6 * 2 * HDEV * D, transcendentals=1024 * HDEV
        ),
    )(tokens, cotangent, routes.T, route_slots.T, route_gates.T, w_gate, w_up, w_down)


def solution(mesh):
    spec = P(("node", "local"), None)
    return jax.shard_map(
        per_device, mesh=mesh, in_specs=(spec,) * 8, out_specs=(spec,) * 4, check_vma=False
    )
```

```python
import jax
import jax.numpy as jnp
from jax import lax
from jax.experimental import pallas as pl
from jax.experimental.pallas import tpu as pltpu
from jax.sharding import PartitionSpec as P

MESH = pl.DeviceIdType.MESH
BF16, F32 = jnp.bfloat16, jnp.float32
CAP = 8
TOK = 128
D = 3584
HDEV = 512
BLK = 16
ROWS = 256
HALF = 128
TILE = 512
NT = (((1,), (1,)), ((), ()))
NN = (((1,), (0,)), ((), ()))
STEPS = (
    (0, 0), (1, 0), (0, 1), (3, 0), (0, 3), (1, 1), (3, 3), (1, 3),
    (3, 1), (2, 0), (0, 2), (2, 1), (1, 2), (2, 3), (3, 2), (2, 2),
)
X_STEPS = sum(dx << (2 * q) for q, (dx, _) in enumerate(STEPS))
Y_STEPS = sum(dy << (2 * q) for q, (_, dy) in enumerate(STEPS))
PLACE = {0: (0, 128), 1: (256, 512), 3: (384, 640), 2: (768, 896)}
WHOLE = ((0, D),)
PIECES = ((0, 1536), (1536, 1024), (2560, 1024))


def signed(v):
    return v - (1 << 32) if v >= 1 << 31 else v


def mm(a, b, dims=NN):
    return lax.dot_general(a, b, dims, preferred_element_type=F32)


def mod4(v):
    return lax.rem(v, 4)


def tiled(body, start=0, size=D):
    def step(t, carry):
        body(pl.ds(pl.multiple_of(start + t * TILE, TILE), TILE))
        return carry

    lax.fori_loop(0, size // TILE, step, 0)


def place(d, q):
    return PLACE[d][q // 8] + q % 8 * BLK


def kernel(
    tok, cot, routes, slots, gates, wg_h, wu_h, wd_h,
    out_tok, out_last, out_rest, og_h, ou_h, od_h,
    wg, wu, wd, xs, gs, snd, toks, cots, meta, onehot, picks, ret,
    swap_snd, swap_rcv, sum_snd, sum_rcv, ht, ggt, ugt, gg, ug, stage,
    w_sem, l_sem, cx_send, cx_recv, m_send, m_recv, own_sem, d_send, d_recv,
    z_send, z_recv, f_send, f_recv, r_send, r_recv, rown_sem,
    t_send, t_recv, o_send, o_recv, st_sem,
):
    node, local = lax.axis_index("node"), lax.axis_index("local")
    y, c = lax.div(node, 2), lax.rem(node, 2)
    x, z = lax.div(local, 4), lax.rem(local, 4)

    def dev(dx, dy, dz, flip=False):
        core = 1 - c if flip else c
        return (mod4(y + dy) * 2 + core, mod4(x + dx) * 4 + mod4(z + dz))

    def remote(src, dst, ssem, rsem, target):
        return pltpu.make_async_remote_copy(
            src_ref=src, dst_ref=dst, send_sem=ssem, recv_sem=rsem,
            device_id=target, device_id_type=MESH,
        )

    here = dev(0, 0, 0, True)

    def wait_recv(ref, sem):
        remote(ref, ref, sem, sem, here).wait_recv()

    def wait_send(ref, sem):
        remote(ref, ref, sem, sem, here).wait_send()

    mine = pl.ds(pl.multiple_of(c * TOK, TOK), TOK)
    own_loads = [
        pltpu.make_async_copy(src, dst.at[mine], l_sem.at[k])
        for k, (src, dst) in enumerate(((tok, toks), (cot, cots)))
    ]
    loads = [
        pltpu.make_async_copy(src, dst, w_sem.at[k])
        for k, (src, dst) in enumerate(((wg_h, wg), (wu_h, wu), (wd_h, wd)))
    ]
    for load in own_loads + loads:
        load.start()

    barrier = pltpu.get_barrier_semaphore()

    def greet(target):
        pl.semaphore_signal(barrier, inc=1, device_id=target, device_id_type=MESH)

    greet(here)
    for dx, dy in STEPS[1:]:
        greet(dev(dx, dy, 0))
    for dz in (1, 2, 3):
        greet(dev(0, 0, dz))

    line = lax.broadcasted_iota(jnp.int32, (8, TOK), 0)
    target = jnp.where(slots[...] < CAP, routes[...] * CAP + slots[...], -1).astype(F32)
    gate = gates[...]
    meta[0, c] = jnp.where(
        line == 0, target[0:1, :],
        jnp.where(line == 1, target[1:2, :], jnp.where(line == 2, gate[0:1, :], gate[1:2, :])),
    )
    pl.semaphore_wait(barrier, 19)

    swaps = [
        remote(src, dst, cx_send.at[k], cx_recv.at[k], here)
        for k, (src, dst) in enumerate(
            ((meta.at[0, c], meta.at[0, c]), (tok, toks.at[mine]), (cot, cots.at[mine]))
        )
    ]
    for swap in swaps:
        swap.start()

    def row_target(r, core):
        q2 = (r >> 4) * 2
        ey = mod4(y + ((jnp.int32(signed(Y_STEPS)) >> q2) & 3))
        ex = mod4(x + ((jnp.int32(signed(X_STEPS)) >> q2) & 3))
        e = (ey * 2 + c) * 4 + ex
        return jnp.where(((r >> 3) & 1) == core, e * CAP + (r & 7), -2).astype(F32)

    swaps[0].wait_recv()
    metas = [
        remote(meta.at[0], meta.at[4 - dz], m_send.at[dz - 1], m_recv.at[3 - dz], dev(0, 0, dz))
        for dz in (1, 2, 3)
    ]
    for m in metas:
        m.start()

    row_ids = lax.broadcasted_iota(jnp.int32, (ROWS, TOK), 0)
    row_gate = jnp.zeros((ROWS, 1), F32)
    for core in (0, 1):
        want = row_target(row_ids, core)
        mt = meta[0, core]
        hit0, hit1 = want == mt[0:1, :], want == mt[1:2, :]
        onehot[:, pl.ds(core * TOK, TOK)] = (
            jnp.where(hit0, 1.0, 0.0) + jnp.where(hit1, 1.0, 0.0)
        ).astype(BF16)
        picked = jnp.where(hit0, mt[2:3, :], 0.0) + jnp.where(hit1, mt[3:4, :], 0.0)
        row_gate = row_gate + jnp.sum(picked, axis=1, keepdims=True)

    for copy in own_loads:
        copy.wait()
    for swap in swaps[1:]:
        swap.wait_recv()

    bufs = (xs, gs)

    def own_copy(a):
        return pltpu.make_async_copy(
            snd.at[a, pl.ds(0, BLK)], bufs[a].at[pl.ds(0, BLK)], own_sem.at[a]
        )

    for half in range(2):
        rows = pl.ds(half * HALF, HALF)
        half_gate = row_gate[half * HALF : half * HALF + HALF]

        def build(cols, rows=rows, half_gate=half_gate):
            snd[0, rows, cols] = mm(onehot[rows, :], toks[:, cols]).astype(BF16)
            snd[1, rows, cols] = (half_gate * mm(onehot[rows, :], cots[:, cols])).astype(BF16)

        tiled(build)
        for q in range(half * 8, half * 8 + 8):
            dx, dy = STEPS[q]
            for a in range(2):
                if q == 0:
                    own_copy(a).start()
                else:
                    remote(
                        snd.at[a, pl.ds(q * BLK, BLK)], bufs[a].at[pl.ds(place(0, q), BLK)],
                        d_send.at[a], d_recv.at[q], dev(dx, dy, 0),
                    ).start()

    for q in range(16):
        if q == 0:
            for a in range(2):
                own_copy(a).wait()
        else:
            wait_recv(xs.at[pl.ds(0, 2 * BLK)], d_recv.at[q])
        for dz, slot in ((1, 3), (3, 1)):
            for a in range(2):
                remote(
                    bufs[a].at[pl.ds(place(0, q), BLK)], bufs[a].at[pl.ds(place(slot, q), BLK)],
                    z_send.at[dz // 2], z_recv.at[slot // 2, q], dev(0, 0, dz),
                ).start()

    def forward(q):
        for a, slot, dz in ((0, 3, 1), (1, 1, 3)):
            wait_recv(xs.at[pl.ds(0, 2 * BLK)], z_recv.at[slot // 2, q])
            remote(
                bufs[a].at[pl.ds(place(slot, q), BLK)], bufs[a].at[pl.ds(place(2, q), BLK)],
                f_send.at[a], f_recv.at[q], dev(0, 0, dz),
            ).start()

    def hidden_pass(row, count, at):
        rows, to = pl.ds(row, count), pl.ds(at, count)

        def step(h, carry):
            hid = pl.ds(pl.multiple_of(h * 256, 256), 256)
            pre_gate = mm(wg[hid, :], xs[rows, :], NT)
            pre_up = mm(wu[hid, :], xs[rows, :], NT)
            hidden_grad = mm(wd[hid, :], gs[rows, :], NT)
            sig = jax.nn.sigmoid(pre_gate)
            active = pre_gate * sig
            ht[hid, rows] = (active * pre_up).astype(BF16)
            gate_grad = hidden_grad * pre_up * sig * (1.0 + pre_gate * (1.0 - sig))
            up_grad = hidden_grad * active
            ggt[hid, rows] = gate_grad.astype(BF16)
            ugt[hid, rows] = up_grad.astype(BF16)
            gg[to, hid] = gate_grad.T.astype(BF16)
            ug[to, hid] = up_grad.T.astype(BF16)
            return carry

        lax.fori_loop(0, HDEV // 256, step, 0)

    def give_back(slot, at, count, blocks, sem, start=0, size=D):
        to = pl.ds(at, count)

        def part(cols):
            snd[slot, to, cols] = (
                mm(gg[to, :], wg[:, cols]) + mm(ug[to, :], wu[:, cols])
            ).astype(BF16)

        tiled(part, start, size)
        cols = pl.ds(start, size)
        own = []
        for row, d, q in blocks:
            src = snd.at[slot, pl.ds(row, BLK), cols]
            dst = ret.at[pl.ds(d * ROWS + q * BLK, BLK), cols]
            if q == 0:
                own.append(pltpu.make_async_copy(src, dst, rown_sem.at[d]))
                own[-1].start()
            else:
                dx, dy = STEPS[q]
                remote(
                    src, dst, r_send.at[sem], r_recv.at[d, sem], dev(4 - dx, 4 - dy, 0)
                ).start()
        for copy in own:
            copy.wait()

    def part_ids(d):
        return (3, 4, 5) if d == 2 else (d // 2 + (d > 0),)

    def spans(d):
        return PIECES if d == 2 else WHOLE

    def swap_copy(d, k):
        cols, i = pl.ds(*spans(d)[k]), part_ids(d)[k]
        return remote(
            swap_snd.at[d, :, cols], swap_rcv.at[d, :, cols], t_send.at[i], t_recv.at[i], here
        )

    def stays(d, k):
        return d > 0 and (d, k) != (2, 2)

    def sum_copy(d, k):
        cols, i, o = pl.ds(*spans(d)[k]), part_ids(d)[k], part_ids((4 - d) % 4)[k]
        return remote(
            sum_snd.at[d, :, cols], sum_rcv.at[3 - d, :, cols],
            o_send.at[i], o_recv.at[o], dev(0, 0, d),
        )

    def prepare(d):
        if d:
            wait_recv(meta.at[d], m_recv.at[d - 1])
        col_ids = lax.broadcasted_iota(jnp.int32, (TOK, ROWS), 1)
        for k, core in enumerate((c, 1 - c)):
            want = row_target(col_ids, core)
            m = meta[d, core].T
            pick = jnp.where(want == m[:, 0:1], 1.0, 0.0) + jnp.where(want == m[:, 1:2], 1.0, 0.0)
            picks[d, k] = pick.astype(BF16)

    def combine(d, k):
        start, size = spans(d)[k]

        def sums(cols):
            rows = ret[pl.ds(d * ROWS, ROWS), cols]
            sum_snd[d, :, cols] = mm(picks[d, 0], rows).astype(BF16)
            swap_snd[d, :, cols] = mm(picks[d, 1], rows).astype(BF16)

        tiled(sums, start, size)
        swap_copy(d, k).start()

    def pass_on(d, k):
        start, size = spans(d)[k]
        swap_copy(d, k).wait_recv()

        def add(cols):
            both = sum_snd[d, :, cols].astype(F32) + swap_rcv[d, :, cols].astype(F32)
            sum_snd[d, :, cols] = both.astype(BF16)

        if (d, k) == (2, 2):
            def add(cols):
                both = sum_snd[d, :, cols].astype(F32) + swap_rcv[d, :, cols].astype(F32)
                out_last[:, pl.ds(cols.start - start, TILE)] = both.astype(BF16)

        tiled(add, start, size)
        if stays(d, k):
            sum_copy(d, k).start()

    def wait_back(d, rows, sem, start=0, size=D):
        wait_recv(ret.at[pl.ds(0, rows), pl.ds(start, size)], r_recv.at[d, sem])

    for q in range(8):
        forward(q)
    for load in loads:
        load.wait()
    for a in range(2):
        wait_send(snd.at[a, pl.ds(0, 240)], d_send.at[a])
    hidden_pass(0, ROWS, 0)
    give_back(0, 0, ROWS, [(q * BLK, 0, q) for q in range(16)], 0)
    hidden_pass(256, ROWS, 0)
    near = [(q % 8 * BLK + k * HALF, d, q) for k, d in enumerate((1, 3)) for q in range(16)]
    give_back(1, 0, ROWS, [b for b in near if b[2] < 8], 1)
    for d in range(4):
        prepare(d)
    for q in range(8, 16):
        forward(q)

    wait_send(snd.at[0, pl.ds(0, 240)], r_send.at[0])
    hidden_pass(512, ROWS, 0)
    give_back(0, 0, ROWS, [b for b in near if b[2] >= 8], 2)
    wait_back(0, 240, 0)
    combine(0, 0)

    for q in range(8):
        wait_recv(xs.at[pl.ds(0, 2 * BLK)], f_recv.at[q])
    pass_on(0, 0)
    wait_send(snd.at[1, pl.ds(0, 224)], r_send.at[1])
    hidden_pass(768, HALF, 0)
    give_back(1, 0, HALF, [(q * BLK, 2, q) for q in range(8)], 3)
    for d in (1, 3):
        wait_back(d, 112, 1)
        wait_back(d, 128, 2)
        combine(d, 0)
    for d in (1, 3):
        pass_on(d, 0)
    for q in range(8, 16):
        wait_recv(xs.at[pl.ds(0, 2 * BLK)], f_recv.at[q])
    hidden_pass(896, HALF, HALF)
    for k, span in enumerate(PIECES):
        give_back(1, HALF, HALF, [(q * BLK, 2, q) for q in range(8, 16)], 4 + k, *span)

    jobs = ((ggt, xs, og_h), (ugt, xs, ou_h), (ht, gs, od_h))

    def stage_copy(t, n):
        return pltpu.make_async_copy(
            stage.at[t % 2, n], jobs[n][2].at[:, pl.ds(t * TILE, TILE)], st_sem.at[t % 2, n]
        )

    def wgrad(t):
        for n, (left, right, _) in enumerate(jobs):
            if t >= 2:
                stage_copy(t - 2, n).wait()
            stage[t % 2, n] = mm(left[...], right[:, pl.ds(t * TILE, TILE)]).astype(BF16)
            stage_copy(t, n).start()

    def last(k):
        if k == 0:
            wait_back(2, 112, 3)
        wait_back(2, 128, 4 + k, *PIECES[k])
        combine(2, k)

    wgrad(0)
    wgrad(1)
    wgrad(2)
    last(0)
    wgrad(3)
    pass_on(2, 0)
    last(1)
    wgrad(4)
    pass_on(2, 1)
    last(2)
    wgrad(5)
    pass_on(2, 2)
    wgrad(6)

    for d in (1, 3):
        wait_recv(sum_rcv.at[d - 1], o_recv.at[part_ids(d)[0]])
    for k, (start, size) in enumerate(PIECES):
        if k < 2:
            wait_recv(sum_rcv.at[1, :, pl.ds(start, size)], o_recv.at[part_ids(2)[k]])

        def total(cols, k=k):
            acc = sum_snd[0, :, cols].astype(F32)
            for n in (0, 1, 2) if k < 2 else (0, 2):
                acc = acc + sum_rcv[n, :, cols].astype(F32)
            if k < 2:
                out_tok[:, cols] = acc.astype(BF16)
            else:
                out_rest[:, pl.ds(cols.start - start, TILE)] = acc

        tiled(total, start, size)

    for t in (5, 6):
        for n in range(3):
            stage_copy(t, n).wait()
    for swap in swaps:
        swap.wait_send()
    for m in metas:
        m.wait_send()
    for k in range(2):
        wait_send(xs.at[pl.ds(0, 512)], z_send.at[k])
        wait_send(xs.at[pl.ds(0, ROWS)], f_send.at[k])
    wait_send(snd.at[0, pl.ds(0, ROWS)], r_send.at[2])
    wait_send(snd.at[0, pl.ds(0, 112)], r_send.at[3])
    for k, (start, size) in enumerate(PIECES):
        wait_send(snd.at[0, pl.ds(0, HALF), pl.ds(start, size)], r_send.at[4 + k])
    for d in range(4):
        for k in range(len(spans(d))):
            swap_copy(d, k).wait_send()
            if stays(d, k):
                sum_copy(d, k).wait_send()


def hand_over(a_in, b_in, c_in, a_out, b_out, c_out, held, in_sem, out_sem):
    ways = []
    for n, (src, dst) in enumerate(((a_in, a_out), (b_in, b_out), (c_in, c_out))):
        for k in range(4):
            rows, slot = pl.ds(k * HALF, HALF), held.at[n, k]
            ways.append((
                pltpu.make_async_copy(src.at[rows], slot, in_sem.at[n, k]),
                pltpu.make_async_copy(slot, dst.at[rows], out_sem.at[n, k]),
            ))
    for enter, _ in ways:
        enter.start()
    for enter, leave in ways:
        enter.wait()
        leave.start()
    for _, leave in ways:
        leave.wait()


def per_device(tokens, cotangent, routes, route_gates, route_slots, w_gate, w_up, w_down):
    vmem, hbm = pl.BlockSpec(memory_space=pltpu.VMEM), pl.BlockSpec(memory_space=pl.ANY)
    dma = pltpu.SemaphoreType.DMA
    grad = jax.ShapeDtypeStruct((HDEV, D), BF16)

    def room(*shape):
        return pltpu.VMEM(shape, BF16)

    start, size = PIECES[2]
    done, last, rest, *grads = pl.pallas_call(
        kernel,
        out_shape=(
            jax.ShapeDtypeStruct((TOK, start), BF16),
            jax.ShapeDtypeStruct((TOK, size), BF16),
            jax.ShapeDtypeStruct((TOK, size), F32),
            grad, grad, grad,
        ),
        in_specs=[hbm] * 2 + [vmem] * 3 + [hbm] * 3,
        out_specs=(vmem, vmem, vmem, hbm, hbm, hbm),
        scratch_shapes=[
            room(HDEV, D), room(HDEV, D), room(HDEV, D),
            room(4 * ROWS, D), room(4 * ROWS, D), room(2, ROWS, D),
            room(2 * TOK, D), room(2 * TOK, D),
            pltpu.VMEM((4, 2, 8, TOK), F32), room(ROWS, 2 * TOK), room(4, 2, TOK, ROWS),
            room(4 * ROWS, D),
            room(4, TOK, D), room(4, TOK, D), room(4, TOK, D), room(3, TOK, D),
            room(HDEV, 4 * ROWS), room(HDEV, 4 * ROWS), room(HDEV, 4 * ROWS),
            room(ROWS, HDEV), room(ROWS, HDEV), room(2, 3, HDEV, TILE),
            dma((3,)), dma((2,)), dma((3,)), dma((3,)), dma((3,)), dma((3,)), dma((2,)),
            dma((2,)), dma((16,)),
            dma((2,)), dma((2, 16)), dma((2,)), dma((16,)), dma((7,)), dma((4, 7)), dma((4,)),
            dma((6,)), dma((6,)), dma((6,)), dma((6,)), dma((2, 3)),
        ],
        compiler_params=pltpu.CompilerParams(
            collective_id=0, has_side_effects=True, vmem_limit_bytes=63 * 2**20
        ),
        cost_estimate=pl.CostEstimate(
            flops=8 * 2 * 1024 * D * HDEV, bytes_accessed=6 * 2 * HDEV * D, transcendentals=1024 * HDEV
        ),
    )(tokens, cotangent, routes.T, route_slots.T, route_gates.T, w_gate, w_up, w_down)
    opposite = [(i, i // 4 * 4 + (i + 2) % 4) for i in range(16)]
    far = lax.ppermute(last, "local", opposite)
    grads = pl.pallas_call(
        hand_over,
        out_shape=(grad, grad, grad),
        in_specs=[hbm] * 3,
        out_specs=[hbm] * 3,
        scratch_shapes=[room(3, 4, HALF, D), dma((3, 4)), dma((3, 4))],
        compiler_params=pltpu.CompilerParams(vmem_limit_bytes=63 * 2**20),
        cost_estimate=pl.CostEstimate(
            flops=0, bytes_accessed=6 * 2 * HDEV * D, transcendentals=0
        ),
    )(*grads)
    tail = (rest + far.astype(F32)).astype(BF16)
    return (jnp.concatenate([done, tail], axis=1), *grads)


def solution(mesh):
    spec = P(("node", "local"), None)
    return jax.shard_map(
        per_device, mesh=mesh, in_specs=(spec,) * 8, out_specs=(spec,) * 4, check_vma=False
    )
```

```python
import jax
import jax.numpy as jnp
from jax import lax
from jax.experimental import pallas as pl
from jax.experimental.pallas import tpu as pltpu
from jax.sharding import PartitionSpec as P

MESH = pl.DeviceIdType.MESH
BF16, F32 = jnp.bfloat16, jnp.float32
CAP = 8
TOK = 128
D = 3584
HDEV = 512
BLK = 16
ROWS = 256
HALF = 128
TILE = 512
NT = (((1,), (1,)), ((), ()))
NN = (((1,), (0,)), ((), ()))
STEPS = (
    (0, 0), (1, 0), (0, 1), (3, 0), (0, 3), (1, 1), (3, 3), (1, 3),
    (3, 1), (2, 0), (0, 2), (2, 1), (1, 2), (2, 3), (3, 2), (2, 2),
)
X_STEPS = sum(dx << (2 * q) for q, (dx, _) in enumerate(STEPS))
Y_STEPS = sum(dy << (2 * q) for q, (_, dy) in enumerate(STEPS))
WHOLE = ((0, D),)
PIECES = ((0, 1536), (1536, 1024), (2560, 1024))
LEAVE = 2560
ENTRY = ((0, 1536), (1536, 2048))


def signed(v):
    return v - (1 << 32) if v >= 1 << 31 else v


def mm(a, b, dims=NN):
    return lax.dot_general(a, b, dims, preferred_element_type=F32)


def mod4(v):
    return lax.rem(v, 4)


def tiled(body, start=0, size=D):
    def step(t, carry):
        body(pl.ds(pl.multiple_of(start + t * TILE, TILE), TILE))
        return carry

    lax.fori_loop(0, size // TILE, step, 0)


def place(d, q):
    if d in (0, 2):
        return d * 384 + q * BLK
    if q < 8:
        return 256 + d // 2 * HALF + q * BLK
    return 512 + (q - 8) // 4 * HALF + d // 2 * 64 + q % 4 * BLK


def kernel(
    tok, cot, routes, slots, gates, wg_h, wu_h, wd_h,
    out_tok, out_last, out_rest, og_h, ou_h, od_h,
    wg, wu, wd, xs, gs, snd, toks, cots, meta, onehot, picks, ret,
    swap_snd, swap_rcv, sum_snd, sum_rcv, ht, ggt, ugt, gg, ug, stage,
    w_sem, l_sem, cx_send, cx_recv, m_send, m_recv, own_sem, d_send, d_recv,
    z_send, z_recv, f_send, f_recv, r_send, r_recv, rown_sem,
    t_send, t_recv, o_send, o_recv, st_sem,
):
    node, local = lax.axis_index("node"), lax.axis_index("local")
    y, c = lax.div(node, 2), lax.rem(node, 2)
    x, z = lax.div(local, 4), lax.rem(local, 4)

    def dev(dx, dy, dz, flip=False):
        core = 1 - c if flip else c
        return (mod4(y + dy) * 2 + core, mod4(x + dx) * 4 + mod4(z + dz))

    def remote(src, dst, ssem, rsem, target):
        return pltpu.make_async_remote_copy(
            src_ref=src, dst_ref=dst, send_sem=ssem, recv_sem=rsem,
            device_id=target, device_id_type=MESH,
        )

    here = dev(0, 0, 0, True)

    def wait_recv(ref, sem):
        remote(ref, ref, sem, sem, here).wait_recv()

    def wait_send(ref, sem):
        remote(ref, ref, sem, sem, here).wait_send()

    mine = pl.ds(pl.multiple_of(c * TOK, TOK), TOK)
    own_loads = [
        pltpu.make_async_copy(src, dst.at[mine], l_sem.at[k])
        for k, (src, dst) in enumerate(((tok, toks), (cot, cots)))
    ]
    loads = [
        pltpu.make_async_copy(src, dst, w_sem.at[k])
        for k, (src, dst) in enumerate(((wg_h, wg), (wu_h, wu), (wd_h, wd)))
    ]
    for load in own_loads + loads:
        load.start()

    barrier = pltpu.get_barrier_semaphore()

    def greet(target):
        pl.semaphore_signal(barrier, inc=1, device_id=target, device_id_type=MESH)

    greet(here)
    for dx, dy in STEPS[1:]:
        greet(dev(dx, dy, 0))
    for dz in (1, 2, 3):
        greet(dev(0, 0, dz))

    line = lax.broadcasted_iota(jnp.int32, (8, TOK), 0)
    target = jnp.where(slots[...] < CAP, routes[...] * CAP + slots[...], -1).astype(F32)
    gate = gates[...]
    meta[0, c] = jnp.where(
        line == 0, target[0:1, :],
        jnp.where(line == 1, target[1:2, :], jnp.where(line == 2, gate[0:1, :], gate[1:2, :])),
    )
    pl.semaphore_wait(barrier, 19)

    swaps = [
        remote(src, dst, cx_send.at[k], cx_recv.at[k], here)
        for k, (src, dst) in enumerate(
            [(meta.at[0, c], meta.at[0, c])]
            + [
                (src.at[:, pl.ds(*span)], dst.at[mine, pl.ds(*span)])
                for span in ENTRY
                for src, dst in ((tok, toks), (cot, cots))
            ]
        )
    ]
    for swap in swaps:
        swap.start()

    def row_target(r, core):
        q2 = (r >> 4) * 2
        ey = mod4(y + ((jnp.int32(signed(Y_STEPS)) >> q2) & 3))
        ex = mod4(x + ((jnp.int32(signed(X_STEPS)) >> q2) & 3))
        e = (ey * 2 + c) * 4 + ex
        return jnp.where(((r >> 3) & 1) == core, e * CAP + (r & 7), -2).astype(F32)

    swaps[0].wait_recv()
    metas = [
        remote(meta.at[0], meta.at[4 - dz], m_send.at[dz - 1], m_recv.at[3 - dz], dev(0, 0, dz))
        for dz in (1, 2, 3)
    ]
    for m in metas:
        m.start()

    row_ids = lax.broadcasted_iota(jnp.int32, (ROWS, TOK), 0)
    row_gate = jnp.zeros((ROWS, 1), F32)
    for core in (0, 1):
        want = row_target(row_ids, core)
        mt = meta[0, core]
        hit0, hit1 = want == mt[0:1, :], want == mt[1:2, :]
        onehot[:, pl.ds(core * TOK, TOK)] = (
            jnp.where(hit0, 1.0, 0.0) + jnp.where(hit1, 1.0, 0.0)
        ).astype(BF16)
        picked = jnp.where(hit0, mt[2:3, :], 0.0) + jnp.where(hit1, mt[3:4, :], 0.0)
        row_gate = row_gate + jnp.sum(picked, axis=1, keepdims=True)

    for copy in own_loads:
        copy.wait()
    bufs = (xs, gs)

    def own_copy(a):
        return pltpu.make_async_copy(
            snd.at[a, pl.ds(0, BLK)], bufs[a].at[pl.ds(0, BLK)], own_sem.at[a]
        )

    for half in range(2):
        rows = pl.ds(half * HALF, HALF)
        half_gate = row_gate[half * HALF : half * HALF + HALF]

        def build(cols, rows=rows, half_gate=half_gate):
            snd[0, rows, cols] = mm(onehot[rows, :], toks[:, cols]).astype(BF16)
            snd[1, rows, cols] = (half_gate * mm(onehot[rows, :], cots[:, cols])).astype(BF16)

        for n, span in enumerate(ENTRY):
            if half == 0:
                for swap in swaps[1 + 2 * n : 3 + 2 * n]:
                    swap.wait_recv()
            tiled(build, *span)
        for q in range(half * 8, half * 8 + 8):
            dx, dy = STEPS[q]
            for a in range(2):
                if q == 0:
                    own_copy(a).start()
                else:
                    remote(
                        snd.at[a, pl.ds(q * BLK, BLK)], bufs[a].at[pl.ds(place(0, q), BLK)],
                        d_send.at[a], d_recv.at[q], dev(dx, dy, 0),
                    ).start()

    for q in range(16):
        if q == 0:
            for a in range(2):
                own_copy(a).wait()
        else:
            wait_recv(xs.at[pl.ds(0, 2 * BLK)], d_recv.at[q])
        for dz, slot in ((1, 3), (3, 1)):
            if q >= 8:
                wait_send(xs.at[pl.ds(0, 2 * BLK)], z_send.at[dz // 2, q - 8])
            for a in range(2):
                remote(
                    bufs[a].at[pl.ds(place(0, q), BLK)], bufs[a].at[pl.ds(place(slot, q), BLK)],
                    z_send.at[dz // 2, q], z_recv.at[slot // 2, q], dev(0, 0, dz),
                ).start()

    def wait_near(q):
        for k in range(2):
            wait_recv(xs.at[pl.ds(0, 2 * BLK)], z_recv.at[k, q])

    def forward(q):
        for a, slot, dz in ((0, 3, 1), (1, 1, 3)):
            remote(
                bufs[a].at[pl.ds(place(slot, q), BLK)], bufs[a].at[pl.ds(place(2, q), BLK)],
                f_send.at[a], f_recv.at[q], dev(0, 0, dz),
            ).start()

    def hidden_pass(row, count, at):
        rows, to = pl.ds(row, count), pl.ds(at, count)

        def step(h, carry):
            hid = pl.ds(pl.multiple_of(h * 256, 256), 256)
            pre_gate = mm(wg[hid, :], xs[rows, :], NT)
            pre_up = mm(wu[hid, :], xs[rows, :], NT)
            hidden_grad = mm(wd[hid, :], gs[rows, :], NT)
            sig = jax.nn.sigmoid(pre_gate)
            active = pre_gate * sig
            ht[hid, rows] = (active * pre_up).astype(BF16)
            gate_grad = hidden_grad * pre_up * sig * (1.0 + pre_gate * (1.0 - sig))
            up_grad = hidden_grad * active
            ggt[hid, rows] = gate_grad.astype(BF16)
            ugt[hid, rows] = up_grad.astype(BF16)
            gg[to, hid] = gate_grad.T.astype(BF16)
            ug[to, hid] = up_grad.T.astype(BF16)
            return carry

        lax.fori_loop(0, HDEV // 256, step, 0)

    def give_back(slot, at, count, blocks, sem, start=0, size=D):
        to = pl.ds(at, count)

        def part(cols):
            snd[slot, to, cols] = (
                mm(gg[to, :], wg[:, cols]) + mm(ug[to, :], wu[:, cols])
            ).astype(BF16)

        tiled(part, start, size)
        cols = pl.ds(start, size)
        own = []
        for row, d, q in blocks:
            src = snd.at[slot, pl.ds(row, BLK), cols]
            dst = ret.at[pl.ds(d * ROWS + q * BLK, BLK), cols]
            if q == 0:
                own.append(pltpu.make_async_copy(src, dst, rown_sem.at[d]))
                own[-1].start()
            else:
                dx, dy = STEPS[q]
                remote(
                    src, dst, r_send.at[sem], r_recv.at[d, sem], dev(4 - dx, 4 - dy, 0)
                ).start()
        for copy in own:
            copy.wait()

    def part_ids(d):
        return (3, 4, 5) if d == 2 else (d // 2 + (d > 0),)

    def spans(d):
        return PIECES if d == 2 else WHOLE

    def swap_copy(d, k):
        cols, i = pl.ds(*spans(d)[k]), part_ids(d)[k]
        return remote(
            swap_snd.at[d, :, cols], swap_rcv.at[d, :, cols], t_send.at[i], t_recv.at[i], here
        )

    def stays(d, k):
        return d > 0 and (d, k) != (2, 2)

    def sum_copy(d, k):
        cols, i, o = pl.ds(*spans(d)[k]), part_ids(d)[k], part_ids((4 - d) % 4)[k]
        return remote(
            sum_snd.at[d, :, cols], sum_rcv.at[3 - d, :, cols],
            o_send.at[i], o_recv.at[o], dev(0, 0, d),
        )

    def prepare(d):
        if d:
            wait_recv(meta.at[d], m_recv.at[d - 1])
        col_ids = lax.broadcasted_iota(jnp.int32, (TOK, ROWS), 1)
        for k, core in enumerate((c, 1 - c)):
            want = row_target(col_ids, core)
            m = meta[d, core].T
            pick = jnp.where(want == m[:, 0:1], 1.0, 0.0) + jnp.where(want == m[:, 1:2], 1.0, 0.0)
            picks[d, k] = pick.astype(BF16)

    def combine(d, k):
        start, size = spans(d)[k]

        def sums(cols):
            rows = ret[pl.ds(d * ROWS, ROWS), cols]
            sum_snd[d, :, cols] = mm(picks[d, 0], rows).astype(BF16)
            swap_snd[d, :, cols] = mm(picks[d, 1], rows).astype(BF16)

        tiled(sums, start, size)
        swap_copy(d, k).start()

    def pass_on(d, k, send=True):
        start, size = spans(d)[k]
        swap_copy(d, k).wait_recv()

        def add(cols):
            both = sum_snd[d, :, cols].astype(F32) + swap_rcv[d, :, cols].astype(F32)
            sum_snd[d, :, cols] = both.astype(BF16)

        if (d, k) == (2, 2):

            def add(cols):
                both = sum_snd[d, :, cols].astype(F32) + swap_rcv[d, :, cols].astype(F32)
                out_last[:, pl.ds(cols.start - LEAVE, TILE)] = both.astype(BF16)

        tiled(add, start, size)
        if send and stays(d, k):
            sum_copy(d, k).start()

    def wait_back(d, rows, sem, start=0, size=D):
        wait_recv(ret.at[pl.ds(0, rows), pl.ds(start, size)], r_recv.at[d, sem])

    for load in loads:
        load.wait()
    for a in range(2):
        wait_send(snd.at[a, pl.ds(0, 240)], d_send.at[a])
    for q in range(8):
        wait_near(q)
    hidden_pass(256, ROWS, 0)
    near = [(place(d, q), d, q) for d in (1, 3) for q in range(16)]
    give_back(1, 0, ROWS, [(row - 256, d, q) for row, d, q in near if row < 512], 1)
    for d in range(4):
        prepare(d)

    for q in range(8, 12):
        wait_near(q)
    hidden_pass(512, HALF, 0)
    give_back(0, 0, HALF, [(row - 512, d, q) for row, d, q in near if 512 <= row < 640], 2)
    hidden_pass(0, HALF, HALF)
    wait_send(snd.at[1, pl.ds(0, 224)], r_send.at[1])
    give_back(1, HALF, HALF, [(HALF + q * BLK, 0, q) for q in range(8)], 0)
    for q in range(12, 16):
        wait_near(q)
        if q >= 14:
            forward(q - 14)
    for q in range(2, 16):
        forward(q)
    hidden_pass(640, HALF, HALF)
    give_back(0, HALF, HALF, [(row - 512, d, q) for row, d, q in near if row >= 640], 7)
    hidden_pass(HALF, HALF, 0)
    give_back(1, 0, HALF, [(q * BLK - HALF, 0, q) for q in range(8, 16)], 8)

    for q in range(8):
        wait_recv(xs.at[pl.ds(0, 2 * BLK)], f_recv.at[q])
    hidden_pass(768, HALF, 0)
    wait_send(snd.at[0, pl.ds(0, HALF)], r_send.at[2])
    give_back(0, 0, HALF, [(q * BLK, 2, q) for q in range(8)], 3)
    for d in (1, 3):
        wait_back(d, 112, 1)
        wait_back(d, 64, 2)
        wait_back(d, 64, 7)
        combine(d, 0)
    for d in (1, 3):
        pass_on(d, 0)
    for q in range(8, 16):
        wait_recv(xs.at[pl.ds(0, 2 * BLK)], f_recv.at[q])
    hidden_pass(896, HALF, HALF)
    wait_send(snd.at[0, pl.ds(0, HALF)], r_send.at[7])
    for k, span in enumerate(PIECES):
        give_back(0, HALF, HALF, [(q * BLK, 2, q) for q in range(8, 16)], 4 + k, *span)

    jobs = ((ggt, xs, og_h), (ugt, xs, ou_h), (ht, gs, od_h))

    def stage_copy(t, n):
        return pltpu.make_async_copy(
            stage.at[t % 2, n], jobs[n][2].at[:, pl.ds(t * TILE, TILE)], st_sem.at[t % 2, n]
        )

    def wgrad(t):
        for n, (left, right, _) in enumerate(jobs):
            if t >= 2:
                stage_copy(t - 2, n).wait()
            stage[t % 2, n] = mm(left[...], right[:, pl.ds(t * TILE, TILE)]).astype(BF16)
            stage_copy(t, n).start()

    def last(k):
        if k == 0:
            wait_back(2, 112, 3)
        wait_back(2, 128, 4 + k, *PIECES[k])
        combine(2, k)

    wgrad(0)
    wait_back(0, 112, 0)
    wait_back(0, 128, 8)
    combine(0, 0)
    wgrad(1)
    pass_on(0, 0)
    wgrad(2)
    last(0)
    wgrad(3)
    pass_on(2, 0)
    last(1)
    wgrad(4)
    pass_on(2, 1)
    last(2)
    pass_on(2, 2)
    wgrad(5)
    wgrad(6)

    for d in (1, 3):
        wait_recv(sum_rcv.at[d - 1], o_recv.at[part_ids(d)[0]])

    def others(cols):
        acc = sum_snd[0, :, cols].astype(F32) + sum_rcv[0, :, cols].astype(F32)
        return acc + sum_rcv[2, :, cols].astype(F32)

    def rest(cols):
        out_rest[:, pl.ds(cols.start - LEAVE, TILE)] = others(cols)

    def total(cols):
        out_tok[:, cols] = (others(cols) + sum_rcv[1, :, cols].astype(F32)).astype(BF16)

    tiled(rest, LEAVE, D - LEAVE)
    for k in range(2):
        start, size = PIECES[k]
        wait_recv(sum_rcv.at[1, :, pl.ds(start, size)], o_recv.at[part_ids(2)[k]])
        tiled(total, start, size)

    for t in (5, 6):
        for n in range(3):
            stage_copy(t, n).wait()
    for swap in swaps:
        swap.wait_send()
    for m in metas:
        m.wait_send()
    for k in range(2):
        for q in range(8, 16):
            wait_send(xs.at[pl.ds(0, 2 * BLK)], z_send.at[k, q])
        wait_send(xs.at[pl.ds(0, ROWS)], f_send.at[k])
    wait_send(snd.at[0, pl.ds(0, 112)], r_send.at[0])
    wait_send(snd.at[0, pl.ds(0, HALF)], r_send.at[8])
    wait_send(snd.at[0, pl.ds(0, 112)], r_send.at[3])
    for k, (start, size) in enumerate(PIECES):
        wait_send(snd.at[0, pl.ds(0, HALF), pl.ds(start, size)], r_send.at[4 + k])
    for d in range(4):
        for k in range(len(spans(d))):
            swap_copy(d, k).wait_send()
            if stays(d, k):
                sum_copy(d, k).wait_send()


def hand_over(a_in, b_in, c_in, a_out, b_out, c_out, held, in_sem, out_sem):
    ways = []
    for n, (src, dst) in enumerate(((a_in, a_out), (b_in, b_out), (c_in, c_out))):
        for k in range(4):
            rows, slot = pl.ds(k * HALF, HALF), held.at[n, k]
            ways.append((
                pltpu.make_async_copy(src.at[rows], slot, in_sem.at[n, k]),
                pltpu.make_async_copy(slot, dst.at[rows], out_sem.at[n, k]),
            ))
    for enter, _ in ways:
        enter.start()
    for enter, leave in ways:
        enter.wait()
        leave.start()
    for _, leave in ways:
        leave.wait()


def per_device(tokens, cotangent, routes, route_gates, route_slots, w_gate, w_up, w_down):
    vmem, hbm = pl.BlockSpec(memory_space=pltpu.VMEM), pl.BlockSpec(memory_space=pl.ANY)
    dma = pltpu.SemaphoreType.DMA
    grad = jax.ShapeDtypeStruct((HDEV, D), BF16)

    def room(*shape):
        return pltpu.VMEM(shape, BF16)

    start, size = LEAVE, D - LEAVE
    done, last, rest, *grads = pl.pallas_call(
        kernel,
        out_shape=(
            jax.ShapeDtypeStruct((TOK, start), BF16),
            jax.ShapeDtypeStruct((TOK, size), BF16),
            jax.ShapeDtypeStruct((TOK, size), F32),
            grad, grad, grad,
        ),
        in_specs=[hbm] * 2 + [vmem] * 3 + [hbm] * 3,
        out_specs=(vmem, vmem, vmem, hbm, hbm, hbm),
        scratch_shapes=[
            room(HDEV, D), room(HDEV, D), room(HDEV, D),
            room(4 * ROWS, D), room(4 * ROWS, D), room(2, ROWS, D),
            room(2 * TOK, D), room(2 * TOK, D),
            pltpu.VMEM((4, 2, 8, TOK), F32), room(ROWS, 2 * TOK), room(4, 2, TOK, ROWS),
            room(4 * ROWS, D),
            room(4, TOK, D), room(4, TOK, D), room(4, TOK, D), room(3, TOK, D),
            room(HDEV, 4 * ROWS), room(HDEV, 4 * ROWS), room(HDEV, 4 * ROWS),
            room(ROWS, HDEV), room(ROWS, HDEV), room(2, 3, HDEV, TILE),
            dma((3,)), dma((2,)), dma((5,)), dma((5,)), dma((3,)), dma((3,)), dma((2,)),
            dma((2,)), dma((16,)),
            dma((2, 16)), dma((2, 16)), dma((2,)), dma((16,)), dma((9,)), dma((4, 9)), dma((4,)),
            dma((6,)), dma((6,)), dma((6,)), dma((6,)), dma((2, 3)),
        ],
        compiler_params=pltpu.CompilerParams(
            collective_id=0, has_side_effects=True, vmem_limit_bytes=63 * 2**20
        ),
        cost_estimate=pl.CostEstimate(
            flops=8 * 2 * 1024 * D * HDEV, bytes_accessed=6 * 2 * HDEV * D, transcendentals=1024 * HDEV
        ),
    )(tokens, cotangent, routes.T, route_slots.T, route_gates.T, w_gate, w_up, w_down)
    opposite = [(i, i // 4 * 4 + (i + 2) % 4) for i in range(16)]
    far = lax.ppermute(last, "local", opposite)
    grads = pl.pallas_call(
        hand_over,
        out_shape=(grad, grad, grad),
        in_specs=[hbm] * 3,
        out_specs=[hbm] * 3,
        scratch_shapes=[room(3, 4, HALF, D), dma((3, 4)), dma((3, 4))],
        compiler_params=pltpu.CompilerParams(vmem_limit_bytes=63 * 2**20),
        cost_estimate=pl.CostEstimate(
            flops=0, bytes_accessed=6 * 2 * HDEV * D, transcendentals=0
        ),
    )(*grads)
    tail = jnp.pad(rest + far.astype(F32), ((0, 0), (start, 0)))
    total = jnp.pad(done.astype(F32), ((0, 0), (0, size))) + tail
    return (total.astype(BF16), *grads)


def solution(mesh):
    spec = P(("node", "local"), None)
    return jax.shard_map(
        per_device, mesh=mesh, in_specs=(spec,) * 8, out_specs=(spec,) * 4, check_vma=False
    )
```

```python
import jax
import jax.numpy as jnp
from jax import lax
from jax.experimental import pallas as pl
from jax.experimental.pallas import tpu as pltpu
from jax.sharding import PartitionSpec as P

MESH = pl.DeviceIdType.MESH
BF16, F32 = jnp.bfloat16, jnp.float32
CAP = 8
TOK = 128
D = 3584
HDEV = 512
BLK = 16
ROWS = 256
HALF = 128
TILE = 512
NT = (((1,), (1,)), ((), ()))
NN = (((1,), (0,)), ((), ()))
STEPS = (
    (0, 0), (1, 0), (0, 1), (3, 0), (0, 3), (1, 1), (3, 3), (1, 3),
    (3, 1), (2, 0), (0, 2), (2, 1), (1, 2), (2, 3), (3, 2), (2, 2),
)
X_STEPS = sum(dx << (2 * q) for q, (dx, _) in enumerate(STEPS))
Y_STEPS = sum(dy << (2 * q) for q, (_, dy) in enumerate(STEPS))
WHOLE = ((0, D),)
PIECES = ((0, 1024), (1024, 1024), (2048, 1536))
LEAVE = 2048
ENTRY = ((0, 1536), (1536, 2048))


def signed(v):
    return v - (1 << 32) if v >= 1 << 31 else v


def mm(a, b, dims=NN):
    return lax.dot_general(a, b, dims, preferred_element_type=F32)


def mod4(v):
    return lax.rem(v, 4)


def tiled(body, start=0, size=D):
    def step(t, carry):
        body(pl.ds(pl.multiple_of(start + t * TILE, TILE), TILE))
        return carry

    lax.fori_loop(0, size // TILE, step, 0)


def place(d, q):
    if d in (0, 2):
        return d * 384 + q * BLK
    if q < 8:
        return 256 + d // 2 * HALF + q * BLK
    return 512 + (q - 8) // 4 * HALF + d // 2 * 64 + q % 4 * BLK


def kernel(
    tok, cot, routes, slots, gates, wg_h, wu_h, wd_h,
    out_tok, out_last, out_rest, og_h, ou_h, od_h,
    wg, wu, wd, xs, gs, snd, toks, cots, meta, onehot, picks, ret,
    swap_snd, swap_rcv, sum_snd, sum_rcv, ht, ggt, ugt, gg, ug, stage,
    w_sem, l_sem, cx_send, cx_recv, m_send, m_recv, own_sem, d_send, d_recv,
    z_send, z_recv, f_send, f_recv, r_send, r_recv, rown_sem,
    t_send, t_recv, o_send, o_recv, st_sem,
):
    node, local = lax.axis_index("node"), lax.axis_index("local")
    y, c = lax.div(node, 2), lax.rem(node, 2)
    x, z = lax.div(local, 4), lax.rem(local, 4)

    def dev(dx, dy, dz, flip=False):
        core = 1 - c if flip else c
        return (mod4(y + dy) * 2 + core, mod4(x + dx) * 4 + mod4(z + dz))

    def remote(src, dst, ssem, rsem, target):
        return pltpu.make_async_remote_copy(
            src_ref=src, dst_ref=dst, send_sem=ssem, recv_sem=rsem,
            device_id=target, device_id_type=MESH,
        )

    here = dev(0, 0, 0, True)

    def wait_recv(ref, sem):
        remote(ref, ref, sem, sem, here).wait_recv()

    def wait_send(ref, sem):
        remote(ref, ref, sem, sem, here).wait_send()

    mine = pl.ds(pl.multiple_of(c * TOK, TOK), TOK)
    own_loads = [
        pltpu.make_async_copy(src, dst.at[mine], l_sem.at[k])
        for k, (src, dst) in enumerate(((tok, toks), (cot, cots)))
    ]
    loads = [
        pltpu.make_async_copy(src, dst, w_sem.at[k])
        for k, (src, dst) in enumerate(((wg_h, wg), (wu_h, wu), (wd_h, wd)))
    ]
    for load in own_loads + loads:
        load.start()

    barrier = pltpu.get_barrier_semaphore()

    def greet(target):
        pl.semaphore_signal(barrier, inc=1, device_id=target, device_id_type=MESH)

    greet(here)
    for dx, dy in STEPS[1:]:
        greet(dev(dx, dy, 0))
    for dz in (1, 2, 3):
        greet(dev(0, 0, dz))

    line = lax.broadcasted_iota(jnp.int32, (8, TOK), 0)
    target = jnp.where(slots[...] < CAP, routes[...] * CAP + slots[...], -1).astype(F32)
    gate = gates[...]
    meta[0, c] = jnp.where(
        line == 0, target[0:1, :],
        jnp.where(line == 1, target[1:2, :], jnp.where(line == 2, gate[0:1, :], gate[1:2, :])),
    )
    pl.semaphore_wait(barrier, 19)

    swaps = [
        remote(src, dst, cx_send.at[k], cx_recv.at[k], here)
        for k, (src, dst) in enumerate(
            [(meta.at[0, c], meta.at[0, c])]
            + [
                (src.at[:, pl.ds(*span)], dst.at[mine, pl.ds(*span)])
                for span in ENTRY
                for src, dst in ((tok, toks), (cot, cots))
            ]
        )
    ]
    for swap in swaps:
        swap.start()

    def row_target(r, core):
        q2 = (r >> 4) * 2
        ey = mod4(y + ((jnp.int32(signed(Y_STEPS)) >> q2) & 3))
        ex = mod4(x + ((jnp.int32(signed(X_STEPS)) >> q2) & 3))
        e = (ey * 2 + c) * 4 + ex
        return jnp.where(((r >> 3) & 1) == core, e * CAP + (r & 7), -2).astype(F32)

    swaps[0].wait_recv()
    metas = [
        remote(meta.at[0], meta.at[4 - dz], m_send.at[dz - 1], m_recv.at[3 - dz], dev(0, 0, dz))
        for dz in (1, 2, 3)
    ]
    for m in metas:
        m.start()

    row_ids = lax.broadcasted_iota(jnp.int32, (ROWS, TOK), 0)
    row_gate = jnp.zeros((ROWS, 1), F32)
    for core in (0, 1):
        want = row_target(row_ids, core)
        mt = meta[0, core]
        hit0, hit1 = want == mt[0:1, :], want == mt[1:2, :]
        onehot[:, pl.ds(core * TOK, TOK)] = (
            jnp.where(hit0, 1.0, 0.0) + jnp.where(hit1, 1.0, 0.0)
        ).astype(BF16)
        picked = jnp.where(hit0, mt[2:3, :], 0.0) + jnp.where(hit1, mt[3:4, :], 0.0)
        row_gate = row_gate + jnp.sum(picked, axis=1, keepdims=True)

    for copy in own_loads:
        copy.wait()
    bufs = (xs, gs)

    def own_copy(a):
        return pltpu.make_async_copy(
            snd.at[a, pl.ds(0, BLK)], bufs[a].at[pl.ds(0, BLK)], own_sem.at[a]
        )

    for half in range(2):
        rows = pl.ds(half * HALF, HALF)
        half_gate = row_gate[half * HALF : half * HALF + HALF]

        def build(cols, rows=rows, half_gate=half_gate):
            snd[0, rows, cols] = mm(onehot[rows, :], toks[:, cols]).astype(BF16)
            snd[1, rows, cols] = (half_gate * mm(onehot[rows, :], cots[:, cols])).astype(BF16)

        for n, span in enumerate(ENTRY):
            if half == 0:
                for swap in swaps[1 + 2 * n : 3 + 2 * n]:
                    swap.wait_recv()
            tiled(build, *span)
        for q in range(half * 8, half * 8 + 8):
            dx, dy = STEPS[q]
            for a in range(2):
                if q == 0:
                    own_copy(a).start()
                else:
                    remote(
                        snd.at[a, pl.ds(q * BLK, BLK)], bufs[a].at[pl.ds(place(0, q), BLK)],
                        d_send.at[a], d_recv.at[q], dev(dx, dy, 0),
                    ).start()

    for q in range(16):
        if q == 0:
            for a in range(2):
                own_copy(a).wait()
        else:
            wait_recv(xs.at[pl.ds(0, 2 * BLK)], d_recv.at[q])
        for dz, slot in ((1, 3), (3, 1)):
            if q >= 8:
                wait_send(xs.at[pl.ds(0, 2 * BLK)], z_send.at[dz // 2, q - 8])
            for a in range(2):
                remote(
                    bufs[a].at[pl.ds(place(0, q), BLK)], bufs[a].at[pl.ds(place(slot, q), BLK)],
                    z_send.at[dz // 2, q], z_recv.at[slot // 2, q], dev(0, 0, dz),
                ).start()

    def wait_near(q):
        for k in range(2):
            wait_recv(xs.at[pl.ds(0, 2 * BLK)], z_recv.at[k, q])

    def forward(q):
        for a, slot, dz in ((0, 3, 1), (1, 1, 3)):
            remote(
                bufs[a].at[pl.ds(place(slot, q), BLK)], bufs[a].at[pl.ds(place(2, q), BLK)],
                f_send.at[a], f_recv.at[q], dev(0, 0, dz),
            ).start()

    def hidden_pass(row, count, at):
        rows, to = pl.ds(row, count), pl.ds(at, count)

        def step(h, carry):
            hid = pl.ds(pl.multiple_of(h * 256, 256), 256)
            pre_gate = mm(wg[hid, :], xs[rows, :], NT)
            pre_up = mm(wu[hid, :], xs[rows, :], NT)
            hidden_grad = mm(wd[hid, :], gs[rows, :], NT)
            sig = jax.nn.sigmoid(pre_gate)
            active = pre_gate * sig
            ht[hid, rows] = (active * pre_up).astype(BF16)
            gate_grad = hidden_grad * pre_up * sig * (1.0 + pre_gate * (1.0 - sig))
            up_grad = hidden_grad * active
            ggt[hid, rows] = gate_grad.astype(BF16)
            ugt[hid, rows] = up_grad.astype(BF16)
            gg[to, hid] = gate_grad.T.astype(BF16)
            ug[to, hid] = up_grad.T.astype(BF16)
            return carry

        lax.fori_loop(0, HDEV // 256, step, 0)

    def give_back(slot, at, count, blocks, sem, start=0, size=D):
        to = pl.ds(at, count)

        def part(cols):
            snd[slot, to, cols] = (
                mm(gg[to, :], wg[:, cols]) + mm(ug[to, :], wu[:, cols])
            ).astype(BF16)

        tiled(part, start, size)
        cols = pl.ds(start, size)
        own = []
        for row, d, q in blocks:
            src = snd.at[slot, pl.ds(row, BLK), cols]
            dst = ret.at[pl.ds(d * ROWS + q * BLK, BLK), cols]
            if q == 0:
                own.append(pltpu.make_async_copy(src, dst, rown_sem.at[d]))
                own[-1].start()
            else:
                dx, dy = STEPS[q]
                remote(
                    src, dst, r_send.at[sem], r_recv.at[d, sem], dev(4 - dx, 4 - dy, 0)
                ).start()
        for copy in own:
            copy.wait()

    def part_ids(d):
        return (3, 4, 5) if d == 2 else (d // 2 + (d > 0),)

    def spans(d):
        return PIECES if d == 2 else WHOLE

    def swap_copy(d, k):
        cols, i = pl.ds(*spans(d)[k]), part_ids(d)[k]
        return remote(
            swap_snd.at[d, :, cols], swap_rcv.at[d, :, cols], t_send.at[i], t_recv.at[i], here
        )

    def stays(d, k):
        return d > 0 and (d, k) != (2, 2)

    def sum_copy(d, k):
        cols, i, o = pl.ds(*spans(d)[k]), part_ids(d)[k], part_ids((4 - d) % 4)[k]
        return remote(
            sum_snd.at[d, :, cols], sum_rcv.at[3 - d, :, cols],
            o_send.at[i], o_recv.at[o], dev(0, 0, d),
        )

    def prepare(d):
        if d:
            wait_recv(meta.at[d], m_recv.at[d - 1])
        col_ids = lax.broadcasted_iota(jnp.int32, (TOK, ROWS), 1)
        for k, core in enumerate((c, 1 - c)):
            want = row_target(col_ids, core)
            m = meta[d, core].T
            pick = jnp.where(want == m[:, 0:1], 1.0, 0.0) + jnp.where(want == m[:, 1:2], 1.0, 0.0)
            picks[d, k] = pick.astype(BF16)

    def combine(d, k):
        start, size = spans(d)[k]

        def sums(cols):
            rows = ret[pl.ds(d * ROWS, ROWS), cols]
            sum_snd[d, :, cols] = mm(picks[d, 0], rows).astype(BF16)
            swap_snd[d, :, cols] = mm(picks[d, 1], rows).astype(BF16)

        tiled(sums, start, size)
        swap_copy(d, k).start()

    def pass_on(d, k, send=True):
        start, size = spans(d)[k]
        swap_copy(d, k).wait_recv()

        def add(cols):
            both = sum_snd[d, :, cols].astype(F32) + swap_rcv[d, :, cols].astype(F32)
            sum_snd[d, :, cols] = both.astype(BF16)

        if (d, k) == (2, 2):

            def add(cols):
                both = sum_snd[d, :, cols].astype(F32) + swap_rcv[d, :, cols].astype(F32)
                out_last[:, pl.ds(cols.start - LEAVE, TILE)] = both.astype(BF16)

        tiled(add, start, size)
        if send and stays(d, k):
            sum_copy(d, k).start()

    def wait_back(d, rows, sem, start=0, size=D):
        wait_recv(ret.at[pl.ds(0, rows), pl.ds(start, size)], r_recv.at[d, sem])

    for load in loads:
        load.wait()
    for a in range(2):
        wait_send(snd.at[a, pl.ds(0, 240)], d_send.at[a])
    for q in range(8):
        wait_near(q)
    hidden_pass(256, ROWS, 0)
    near = [(place(d, q), d, q) for d in (1, 3) for q in range(16)]
    give_back(1, 0, ROWS, [(row - 256, d, q) for row, d, q in near if row < 512], 1)
    for d in range(4):
        prepare(d)

    for q in range(8, 12):
        wait_near(q)
    hidden_pass(512, HALF, 0)
    give_back(0, 0, HALF, [(row - 512, d, q) for row, d, q in near if 512 <= row < 640], 2)
    hidden_pass(0, HALF, HALF)
    wait_send(snd.at[1, pl.ds(0, 224)], r_send.at[1])
    give_back(1, HALF, HALF, [(HALF + q * BLK, 0, q) for q in range(8)], 0)
    for q in range(12, 16):
        wait_near(q)
        if q >= 14:
            forward(q - 14)
    for q in range(2, 16):
        forward(q)
    hidden_pass(640, HALF, HALF)
    give_back(0, HALF, HALF, [(row - 512, d, q) for row, d, q in near if row >= 640], 7)
    hidden_pass(HALF, HALF, 0)
    give_back(1, 0, HALF, [(q * BLK - HALF, 0, q) for q in range(8, 16)], 8)

    for q in range(8):
        wait_recv(xs.at[pl.ds(0, 2 * BLK)], f_recv.at[q])
    hidden_pass(768, HALF, 0)
    wait_send(snd.at[0, pl.ds(0, HALF)], r_send.at[2])
    give_back(0, 0, HALF, [(q * BLK, 2, q) for q in range(8)], 3)
    for d in (1, 3):
        wait_back(d, 112, 1)
        wait_back(d, 64, 2)
        wait_back(d, 64, 7)
        combine(d, 0)
    for d in (1, 3):
        pass_on(d, 0)
    for q in range(8, 16):
        wait_recv(xs.at[pl.ds(0, 2 * BLK)], f_recv.at[q])
    hidden_pass(896, HALF, HALF)
    wait_send(snd.at[0, pl.ds(0, HALF)], r_send.at[7])
    for k, span in enumerate(PIECES):
        give_back(0, HALF, HALF, [(q * BLK, 2, q) for q in range(8, 16)], 4 + k, *span)

    jobs = ((ggt, xs, og_h), (ugt, xs, ou_h), (ht, gs, od_h))

    def stage_copy(t, n):
        return pltpu.make_async_copy(
            stage.at[t % 2, n], jobs[n][2].at[:, pl.ds(t * TILE, TILE)], st_sem.at[t % 2, n]
        )

    def wgrad(t):
        for n, (left, right, _) in enumerate(jobs):
            if t >= 2:
                stage_copy(t - 2, n).wait()
            stage[t % 2, n] = mm(left[...], right[:, pl.ds(t * TILE, TILE)]).astype(BF16)
            stage_copy(t, n).start()

    def last(k):
        if k == 0:
            wait_back(2, 112, 3)
        wait_back(2, 128, 4 + k, *PIECES[k])
        combine(2, k)

    wgrad(0)
    wait_back(0, 112, 0)
    wait_back(0, 128, 8)
    combine(0, 0)
    wgrad(1)
    pass_on(0, 0)
    wgrad(2)
    last(0)
    wgrad(3)
    pass_on(2, 0)
    last(1)
    wgrad(4)
    pass_on(2, 1)
    last(2)
    pass_on(2, 2)
    wgrad(5)
    wgrad(6)

    for d in (1, 3):
        wait_recv(sum_rcv.at[d - 1], o_recv.at[part_ids(d)[0]])

    def others(cols):
        acc = sum_snd[0, :, cols].astype(F32) + sum_rcv[0, :, cols].astype(F32)
        return acc + sum_rcv[2, :, cols].astype(F32)

    def rest(cols):
        out_rest[:, pl.ds(cols.start - LEAVE, TILE)] = others(cols)

    def total(cols):
        out_tok[:, cols] = (others(cols) + sum_rcv[1, :, cols].astype(F32)).astype(BF16)

    tiled(rest, LEAVE, D - LEAVE)
    for k in range(2):
        start, size = PIECES[k]
        wait_recv(sum_rcv.at[1, :, pl.ds(start, size)], o_recv.at[part_ids(2)[k]])
        tiled(total, start, size)

    for t in (5, 6):
        for n in range(3):
            stage_copy(t, n).wait()
    for swap in swaps:
        swap.wait_send()
    for m in metas:
        m.wait_send()
    for k in range(2):
        for q in range(8, 16):
            wait_send(xs.at[pl.ds(0, 2 * BLK)], z_send.at[k, q])
        wait_send(xs.at[pl.ds(0, ROWS)], f_send.at[k])
    wait_send(snd.at[0, pl.ds(0, 112)], r_send.at[0])
    wait_send(snd.at[0, pl.ds(0, HALF)], r_send.at[8])
    wait_send(snd.at[0, pl.ds(0, 112)], r_send.at[3])
    for k, (start, size) in enumerate(PIECES):
        wait_send(snd.at[0, pl.ds(0, HALF), pl.ds(start, size)], r_send.at[4 + k])
    for d in range(4):
        for k in range(len(spans(d))):
            swap_copy(d, k).wait_send()
            if stays(d, k):
                sum_copy(d, k).wait_send()


def hand_over(a_in, b_in, c_in, a_out, b_out, c_out, held, in_sem, out_sem):
    ways = []
    for n, (src, dst) in enumerate(((a_in, a_out), (b_in, b_out), (c_in, c_out))):
        for k in range(4):
            rows, slot = pl.ds(k * HALF, HALF), held.at[n, k]
            ways.append((
                pltpu.make_async_copy(src.at[rows], slot, in_sem.at[n, k]),
                pltpu.make_async_copy(slot, dst.at[rows], out_sem.at[n, k]),
            ))
    for enter, _ in ways:
        enter.start()
    for enter, leave in ways:
        enter.wait()
        leave.start()
    for _, leave in ways:
        leave.wait()


def per_device(tokens, cotangent, routes, route_gates, route_slots, w_gate, w_up, w_down):
    vmem, hbm = pl.BlockSpec(memory_space=pltpu.VMEM), pl.BlockSpec(memory_space=pl.ANY)
    dma = pltpu.SemaphoreType.DMA
    grad = jax.ShapeDtypeStruct((HDEV, D), BF16)

    def room(*shape):
        return pltpu.VMEM(shape, BF16)

    start, size = LEAVE, D - LEAVE
    done, last, rest, *grads = pl.pallas_call(
        kernel,
        out_shape=(
            jax.ShapeDtypeStruct((TOK, start), BF16),
            jax.ShapeDtypeStruct((TOK, size), BF16),
            jax.ShapeDtypeStruct((TOK, size), F32),
            grad, grad, grad,
        ),
        in_specs=[hbm] * 2 + [vmem] * 3 + [hbm] * 3,
        out_specs=(vmem, vmem, vmem, hbm, hbm, hbm),
        scratch_shapes=[
            room(HDEV, D), room(HDEV, D), room(HDEV, D),
            room(4 * ROWS, D), room(4 * ROWS, D), room(2, ROWS, D),
            room(2 * TOK, D), room(2 * TOK, D),
            pltpu.VMEM((4, 2, 8, TOK), F32), room(ROWS, 2 * TOK), room(4, 2, TOK, ROWS),
            room(4 * ROWS, D),
            room(4, TOK, D), room(4, TOK, D), room(4, TOK, D), room(3, TOK, D),
            room(HDEV, 4 * ROWS), room(HDEV, 4 * ROWS), room(HDEV, 4 * ROWS),
            room(ROWS, HDEV), room(ROWS, HDEV), room(2, 3, HDEV, TILE),
            dma((3,)), dma((2,)), dma((5,)), dma((5,)), dma((3,)), dma((3,)), dma((2,)),
            dma((2,)), dma((16,)),
            dma((2, 16)), dma((2, 16)), dma((2,)), dma((16,)), dma((9,)), dma((4, 9)), dma((4,)),
            dma((6,)), dma((6,)), dma((6,)), dma((6,)), dma((2, 3)),
        ],
        compiler_params=pltpu.CompilerParams(
            collective_id=0, has_side_effects=True, vmem_limit_bytes=63 * 2**20
        ),
        cost_estimate=pl.CostEstimate(
            flops=8 * 2 * 1024 * D * HDEV, bytes_accessed=6 * 2 * HDEV * D, transcendentals=1024 * HDEV
        ),
    )(tokens, cotangent, routes.T, route_slots.T, route_gates.T, w_gate, w_up, w_down)
    opposite = [(i, i // 4 * 4 + (i + 2) % 4) for i in range(16)]
    far = lax.ppermute(last, "local", opposite)
    grads = pl.pallas_call(
        hand_over,
        out_shape=(grad, grad, grad),
        in_specs=[hbm] * 3,
        out_specs=[hbm] * 3,
        scratch_shapes=[room(3, 4, HALF, D), dma((3, 4)), dma((3, 4))],
        compiler_params=pltpu.CompilerParams(vmem_limit_bytes=63 * 2**20),
        cost_estimate=pl.CostEstimate(
            flops=0, bytes_accessed=6 * 2 * HDEV * D, transcendentals=0
        ),
    )(*grads)
    tail = jnp.pad(rest + far.astype(F32), ((0, 0), (start, 0)))
    total = jnp.pad(done.astype(F32), ((0, 0), (0, size))) + tail
    return (total.astype(BF16), *grads)


def solution(mesh):
    spec = P(("node", "local"), None)
    return jax.shard_map(
        per_device, mesh=mesh, in_specs=(spec,) * 8, out_specs=(spec,) * 4, check_vma=False
    )
```
